512 devices in a mesh: dp: 2 (over core), row: 64 (over z, y), col: 4 (over x).
Axes of the slice: x: 4, y: 8, z: 8, core: 2. Of those that a mesh axis runs over, the one named last changes fastest.
Arguments:
- grad_in: bfloat16 [2, 4096, 16384], P('dp', 'row', 'col'), may hold values from -50 to 50
- grad_out: bfloat16 [2, 16384, 4096], P('dp', 'row', 'col'), may hold values from -50 to 50
- rows_in: float32 [4096], P('row'), may hold values from 0.05 to 0.5
- cols_in: float32 [16384], P('col'), may hold values from 0.05 to 0.5
- rows_out: float32 [16384], P('row'), may hold values from 0.05 to 0.5
- cols_out: float32 [4096], P('col'), may hold values from 0.05 to 0.5
Outputs:
- update_in: float32 [4096, 16384], P('row', 'col')
- update_out: float32 [16384, 4096], P('row', 'col')
- rows_in_new: float32 [4096], P('row')
- cols_in_new: float32 [16384], P('col')
- rows_out_new: float32 [16384], P('row')
- cols_out_new: float32 [4096], P('col')
The draws below stay inside these ranges and needn't reach their ends.
All inputs are finite; a program needn't handle non-finite values.
Results may differ from the reference program's by a relative error of at most 0.00045.
Values sent between devices are 32-bit elements; how exact they have to be, the bound alone decides.
No kernel may reach another device: no remote copies, remote signals or barrier semaphores. Data moves between devices by JAX's collectives and lax.ppermute only.
A program may use at most 64 MiB of HBM per device.

```python
import math
import jax
import jax.numpy as jnp
from jax import lax

D = 4096
FF = 16384
REPLICAS = 2


def draw_parts(key, height, width):
    key_rows, key_cols, key_noise = jax.random.split(key, 3)
    rise_rows = jnp.arange(height, dtype=jnp.float32) / (height - 1)
    rise_cols = jnp.arange(width, dtype=jnp.float32) / (width - 1)
    row_scale = 10.0 ** (0.5 * jax.random.uniform(key_rows, (height,)) + 0.5 * rise_rows)
    col_scale = 10.0 ** (0.5 * jax.random.uniform(key_cols, (width,)) + 0.5 * rise_cols)
    noise = jnp.clip(jax.random.normal(key_noise, (REPLICAS, height, width)), -5.0, 5.0)
    return 0.1 * noise * row_scale[None, :, None] * col_scale[None, None, :]


def draw_grad_in(key, part):
    key = jax.random.fold_in(key, 1)
    return draw_parts(key, D, FF).astype(jnp.bfloat16)


def draw_grad_out(key, part):
    key = jax.random.fold_in(key, 2)
    return draw_parts(key, FF, D).astype(jnp.bfloat16)


def level_of(rng, extent, cuts, low, high):
    def one(axis_at, blocks):
        heights = jax.random.uniform(jax.random.fold_in(jax.random.fold_in(rng, 6), axis_at), (blocks,), jnp.float32, low / len(cuts), high / len(cuts))
        return jnp.repeat(jnp.exp(heights), extent[axis_at] // blocks).reshape((-1,) + (1,) * (len(extent) - axis_at - 1))

    loudness = one(*cuts[0])
    for cut in cuts[1:]:
        loudness = loudness * one(*cut)
    return loudness


def setup_inputs(seed: int = 0) -> dict:
    arg_keys = jax.random.split(jax.random.key(seed), 7)
    return {
        "grad_in": draw_grad_in(jax.random.fold_in(arg_keys[6], 71), 0),
        "grad_out": draw_grad_out(jax.random.fold_in(arg_keys[6], 71), 0),
        "rows_in": jnp.clip(jnp.exp(math.log(0.5) - 2.3025851 * jax.random.uniform(arg_keys[2], (D,), jnp.float32) ** level_of(arg_keys[2], (D,), ((0, 64),), -0.2, 0.2)), 0.05, 0.5),
        "cols_in": jnp.clip(jnp.exp(math.log(0.5) - 2.3025851 * jax.random.uniform(arg_keys[3], (FF,), jnp.float32) ** level_of(arg_keys[3], (FF,), ((0, 4),), -0.2, 0.2)), 0.05, 0.5),
        "rows_out": jnp.clip(jnp.exp(math.log(0.5) - 2.3025851 * jax.random.uniform(arg_keys[4], (FF,), jnp.float32) ** level_of(arg_keys[4], (FF,), ((0, 64),), -0.2, 0.2)), 0.05, 0.5),
        "cols_out": jnp.clip(jnp.exp(math.log(0.5) - 2.3025851 * jax.random.uniform(arg_keys[5], (D,), jnp.float32) ** level_of(arg_keys[5], (D,), ((0, 4),), -0.2, 0.2)), 0.05, 0.5),
    }


EPSILON = 1e-30
DECAY = 1.0 - 100.0 ** (-0.8)

def factored(parts, rows_old, cols_old):
    summed = parts[0].astype(jnp.float32)
    for index in range(1, REPLICAS):
        summed = summed + parts[index].astype(jnp.float32)
    squares = summed * summed + EPSILON
    rows_new = DECAY * rows_old + (1.0 - DECAY) * lax.optimization_barrier(jnp.mean(squares, axis=1))
    cols_new = DECAY * cols_old + (1.0 - DECAY) * lax.optimization_barrier(jnp.mean(squares, axis=0))
    scaled = summed * lax.rsqrt(rows_new)[:, None] * lax.rsqrt(cols_new)[None, :]
    ratio = jnp.sqrt(jnp.mean(scaled * scaled))
    update = scaled / jnp.maximum(1.0, ratio)
    return (update, rows_new, cols_new)

def reference(grad_in, grad_out, rows_in, cols_in, rows_out, cols_out):
    update_in, rows_in_new, cols_in_new = factored(grad_in, rows_in, cols_in)
    update_out, rows_out_new, cols_out_new = factored(grad_out, rows_out, cols_out)
    return (update_in, update_out, rows_in_new, cols_in_new, rows_out_new, cols_out_new)
```

```python
import jax
import jax.numpy as jnp
from jax import lax
from jax.experimental import pallas as pl
from jax.experimental.pallas import tpu as pltpu
from jax.sharding import Mesh, PartitionSpec as P

D = 4096
FF = 16384

EPSILON = 1e-30
DECAY = 1.0 - 100.0 ** (-0.8)

ROWS_IN, COLS_IN = 64, 4096
ROWS_OUT, COLS_OUT = 256, 1024
HALF_IN, HALF_OUT = COLS_IN // 2, COLS_OUT // 2
PACK = (128, 2048)
BLOCKS = ROWS_OUT // 64
TILES_IN = HALF_IN // 128
TILES_OUT = HALF_OUT // 128

F32 = jnp.float32
VMEM = pl.BlockSpec(memory_space=pltpu.VMEM)
HBM = pl.BlockSpec(memory_space=pl.ANY)
PARAMS = pltpu.CompilerParams(vmem_limit_bytes=16 * 1024 * 1024)


def lanes(tile):
    return pl.ds(tile * 128, 128)


def widen_kernel(other, grad_in, grad_out, packed, buf_in, buf_out, sems):
    half = lax.axis_index("dp")
    if other:
        half = 1 - half
    copy_in = pltpu.make_async_copy(
        grad_in.at[:, pl.ds(pl.multiple_of(half * HALF_IN, 128), HALF_IN)], buf_in, sems.at[0]
    )
    copy_out = pltpu.make_async_copy(
        grad_out.at[:, pl.ds(pl.multiple_of(half * HALF_OUT, 128), HALF_OUT)], buf_out, sems.at[1]
    )
    copy_in.start()
    copy_out.start()
    copy_in.wait()
    packed[0:64, :] = buf_in[...].astype(F32)
    copy_out.wait()
    for k in range(BLOCKS):
        packed[64:128, pl.ds(k * HALF_OUT, HALF_OUT)] = buf_out[pl.ds(64 * k, 64), :].astype(F32)


def widen(other, grad_in, grad_out):
    return pl.pallas_call(
        lambda *refs: widen_kernel(other, *refs),
        out_shape=jax.ShapeDtypeStruct(PACK, F32),
        in_specs=[HBM, HBM],
        out_specs=VMEM,
        scratch_shapes=[
            pltpu.VMEM((ROWS_IN, HALF_IN), jnp.bfloat16),
            pltpu.VMEM((ROWS_OUT, HALF_OUT), jnp.bfloat16),
            pltpu.SemaphoreType.DMA((2,)),
        ],
        compiler_params=PARAMS,
        name="widen_other" if other else "widen_own",
    )(grad_in, grad_out)


def rows_kernel(own, received, summed, row_sums):
    def lane_partial(row, tiles):
        total = None
        for tile in tiles:
            value = own[pl.ds(row, 64), lanes(tile)] + received[pl.ds(row, 64), lanes(tile)]
            summed[pl.ds(row, 64), lanes(tile)] = value
            square = value * value
            total = square if total is None else total + square
        return total

    def to_lanes(upper, lower):
        return jnp.sum(jnp.concatenate([upper, lower], axis=0).T, axis=0, keepdims=True)

    part = lane_partial(0, range(TILES_IN))
    vectors = [to_lanes(part, jnp.zeros_like(part))]
    for pair in range(BLOCKS // 2):
        upper, lower = (
            lane_partial(64, range(k * TILES_OUT, (k + 1) * TILES_OUT)) for k in (2 * pair, 2 * pair + 1)
        )
        vectors.append(to_lanes(upper, lower))
    for at, vector in enumerate(vectors):
        for peer in range(8):
            row_sums[peer, :, lanes(at)] = vector


def row_sums_of(own, received):
    return pl.pallas_call(
        rows_kernel,
        out_shape=(jax.ShapeDtypeStruct(PACK, F32), jax.ShapeDtypeStruct((8, 1, 384), F32)),
        in_specs=[VMEM, VMEM],
        out_specs=(VMEM, VMEM),
        compiler_params=PARAMS,
        name="row_sums",
    )(own, received)


def columns_kernel(row_sums, rows_in, rows_out, summed, scaled, row_scale, new_in, new_out, sends):
    total = jnp.sum(row_sums[...], axis=0)
    fresh_in = DECAY * rows_in[...] + (1.0 - DECAY) * (total[:, 0:64] * (1.0 / FF) + EPSILON)
    fresh_out = DECAY * rows_out[...] + (1.0 - DECAY) * (total[:, 128:384] * (1.0 / D) + EPSILON)
    new_in[...] = fresh_in
    new_out[...] = fresh_out
    root_in = lax.rsqrt(fresh_in)
    root_out = lax.rsqrt(fresh_out)

    def to_rows(vector):
        return jnp.broadcast_to(vector, (128, 128)).T

    row_scale[0:64, :] = to_rows(jnp.concatenate([root_in, root_in], axis=1))[0:64, :]
    row_scale[64:192, :] = to_rows(root_out[:, 0:128])
    row_scale[192:320, :] = to_rows(root_out[:, 128:256])

    def column(row, scale_row, tile):
        value = summed[pl.ds(row, 64), lanes(tile)]
        weighted = value * row_scale[pl.ds(scale_row, 64), :]
        scaled[pl.ds(row, 64), lanes(tile)] = weighted
        return (
            jnp.sum((value * value).reshape(8, 8, 128), axis=0),
            jnp.sum((weighted * weighted).reshape(8, 8, 128), axis=0),
        )

    def fold(value):
        return jnp.sum(value, axis=0, keepdims=True)

    def send(chunk, at, vector):
        for peer in range(8):
            sends[chunk * 8 + peer, :, lanes(at)] = vector

    for tile in range(TILES_IN):
        plain, weighted = column(0, 0, tile)
        send(tile // 2, tile % 2, fold(plain))
        send(tile // 2, 2 + tile % 2, fold(weighted))
    lane = lax.broadcasted_iota(jnp.int32, (1, 128), 1)
    for tile in range(TILES_OUT):
        plain, weighted = column(64, 64, tile)
        for k in range(1, BLOCKS):
            more = column(64, 64 + 64 * k, k * TILES_OUT + tile)
            plain, weighted = plain + more[0], weighted + more[1]
        plain, weighted = fold(plain), fold(weighted)
        send(2 * tile, 4, jnp.where(lane < 64, plain, pltpu.roll(weighted, 64, 1)))
        send(2 * tile + 1, 4, jnp.where(lane < 64, pltpu.roll(plain, 64, 1), weighted))


def column_sums_of(row_sums, rows_in, rows_out, summed):
    return pl.pallas_call(
        columns_kernel,
        out_shape=(
            jax.ShapeDtypeStruct(PACK, F32),
            jax.ShapeDtypeStruct((320, 128), F32),
            jax.ShapeDtypeStruct((1, ROWS_IN), F32),
            jax.ShapeDtypeStruct((1, ROWS_OUT), F32),
            jax.ShapeDtypeStruct((64, 1, 640), F32),
        ),
        in_specs=[VMEM] * 4,
        out_specs=(VMEM,) * 5,
        compiler_params=PARAMS,
        name="column_sums",
    )(row_sums, rows_in, rows_out, summed)


def factors_kernel(sums, cols_in, cols_out, sends):
    owner = lax.axis_index("dp") * 8 + lax.axis_index("z")
    total = jnp.sum(sums[...], axis=0)
    lane = lax.broadcasted_iota(jnp.int32, (1, 128), 1)
    new_in = DECAY * cols_in[owner] + (1.0 - DECAY) * (total[:, 0:256] * (1.0 / D) + EPSILON)
    energy_in = jnp.sum(total[:, 256:512] / new_in, axis=1, keepdims=True)
    mixed = total[:, 512:640]
    old_out = cols_out[owner // 2]
    old_out = jnp.where(owner % 2 == 1, pltpu.roll(old_out, 64, 1), old_out)
    new_out = DECAY * old_out + (1.0 - DECAY) * (mixed * (1.0 / FF) + EPSILON)
    weighted = jnp.where(lane < 64, pltpu.roll(mixed, 64, 1) / new_out, 0.0)
    energy_out = jnp.sum(weighted, axis=1, keepdims=True)
    last = jnp.where(lane < 64, new_out, jnp.where(lane < 96, energy_in, energy_out))
    for peer in range(64):
        sends[peer, :, 0:256] = new_in
        sends[peer, :, 256:384] = last


def factors_of(sums, cols_in, cols_out):
    return pl.pallas_call(
        factors_kernel,
        out_shape=jax.ShapeDtypeStruct((64, 1, 384), F32),
        in_specs=[VMEM] * 3,
        out_specs=VMEM,
        compiler_params=PARAMS,
        name="column_factors",
    )(sums, cols_in, cols_out)


def update_kernel(
    factors, scaled, row_scale, other, received, update_in, update_out, cols_in, cols_out, buf_in, buf_out, sems
):
    own_half = lax.axis_index("dp")
    my_x = lax.axis_index("x")
    lane = lax.broadcasted_iota(jnp.int32, (1, 128), 1)
    energies = jnp.sum(factors[:, :, 256:384], axis=0)

    def limit(at):
        energy = jnp.sum(jnp.where(lane == at, energies, 0.0), axis=1, keepdims=True)
        return 1.0 / jnp.maximum(1.0, jnp.sqrt(energy * (1.0 / (D * FF))))

    limit_in, limit_out = limit(64), limit(96)

    def factor_in(half, tile):
        return factors[(half * 8 + tile // 2) * 4 + my_x, :, lanes(tile % 2)]

    def factor_out(half, tile):
        left = factors[(half * 8 + 2 * tile) * 4 + my_x, :, lanes(2)]
        right = factors[(half * 8 + 2 * tile + 1) * 4 + my_x, :, lanes(2)]
        return jnp.where(lane < 64, left, pltpu.roll(right, 64, 1))

    copies = []
    for which in range(2):
        half = own_half if which == 0 else 1 - own_half

        def value(row, scale_row, tile):
            if which == 0:
                return scaled[pl.ds(row, 64), lanes(tile)]
            both = other[pl.ds(row, 64), lanes(tile)] + received[pl.ds(row, 64), lanes(tile)]
            return both * row_scale[pl.ds(scale_row, 64), :]

        for tile in range(TILES_IN):
            factor = factor_in(half, tile)
            buf_in[which, :, lanes(tile)] = value(0, 0, tile) * (lax.rsqrt(factor) * limit_in)
        copy = pltpu.make_async_copy(
            buf_in.at[which],
            update_in.at[:, pl.ds(pl.multiple_of(half * HALF_IN, 128), HALF_IN)],
            sems.at[2 * which],
        )
        copy.start()
        copies.append(copy)
        for tile in range(TILES_OUT):
            scale = lax.rsqrt(factor_out(half, tile)) * limit_out
            for k in range(BLOCKS):
                buf_out[which, pl.ds(64 * k, 64), lanes(tile)] = (
                    value(64, 64 + 64 * k, k * TILES_OUT + tile) * scale
                )
        copy = pltpu.make_async_copy(
            buf_out.at[which],
            update_out.at[:, pl.ds(pl.multiple_of(half * HALF_OUT, 128), HALF_OUT)],
            sems.at[2 * which + 1],
        )
        copy.start()
        copies.append(copy)
    for half in range(2):
        for tile in range(TILES_IN):
            cols_in[pl.ds(half * TILES_IN + tile, 1), :] = factor_in(half, tile)
        for tile in range(TILES_OUT):
            cols_out[pl.ds(half * TILES_OUT + tile, 1), :] = factor_out(half, tile)
    for copy in copies:
        copy.wait()


def update_of(factors, scaled, row_scale, other, received):
    return pl.pallas_call(
        update_kernel,
        out_shape=(
            jax.ShapeDtypeStruct((ROWS_IN, COLS_IN), F32),
            jax.ShapeDtypeStruct((ROWS_OUT, COLS_OUT), F32),
            jax.ShapeDtypeStruct((COLS_IN // 128, 128), F32),
            jax.ShapeDtypeStruct((COLS_OUT // 128, 128), F32),
        ),
        in_specs=[VMEM] * 5,
        out_specs=(HBM, HBM, VMEM, VMEM),
        scratch_shapes=[
            pltpu.VMEM((2, ROWS_IN, HALF_IN), F32),
            pltpu.VMEM((2, ROWS_OUT, HALF_OUT), F32),
            pltpu.SemaphoreType.DMA((4,)),
        ],
        compiler_params=PARAMS,
        name="update",
    )(factors, scaled, row_scale, other, received)


def per_device(grad_in, grad_out, rows_in, cols_in, rows_out, cols_out):
    grad_in, grad_out = grad_in[0], grad_out[0]
    swap = [(0, 1), (1, 0)]
    other = widen(True, grad_in, grad_out)
    arrived_own = lax.ppermute(other, "dp", swap)
    own = widen(False, grad_in, grad_out)
    arrived_other = lax.ppermute(own, "dp", swap)

    summed, row_sums = row_sums_of(own, arrived_own)
    row_sums = lax.all_to_all(row_sums, ("dp", "x"), 0, 0)
    scaled, row_scale, new_rows_in, new_rows_out, sums = column_sums_of(
        row_sums, rows_in.reshape(1, ROWS_IN), rows_out.reshape(1, ROWS_OUT), summed
    )
    sums = lax.all_to_all(sums, ("z", "y"), 0, 0)
    factors = factors_of(sums, cols_in.reshape(16, 1, 256), cols_out.reshape(8, 1, 128))
    factors = lax.all_to_all(factors, ("dp", "z", "x"), 0, 0)
    update_in, update_out, new_cols_in, new_cols_out = update_of(
        factors, scaled, row_scale, other, arrived_other
    )
    return (
        update_in,
        update_out,
        new_rows_in.reshape(ROWS_IN),
        new_cols_in.reshape(COLS_IN),
        new_rows_out.reshape(ROWS_OUT),
        new_cols_out.reshape(COLS_OUT),
    )


def solution(mesh):
    fine = Mesh(mesh.devices.reshape(2, 8, 8, 4), ("dp", "z", "y", "x"))
    row = ("z", "y")
    return jax.shard_map(
        per_device,
        mesh=fine,
        in_specs=(
            P("dp", row, "x"),
            P("dp", row, "x"),
            P(row),
            P("x"),
            P(row),
            P("x"),
        ),
        out_specs=(P(row, "x"), P(row, "x"), P(row), P("x"), P(row), P("x")),
        check_vma=False,
    )
```

```python
import jax
import jax.numpy as jnp
from jax import lax
from jax.experimental import pallas as pl
from jax.experimental.pallas import tpu as pltpu
from jax.sharding import Mesh, PartitionSpec as P

D = 4096
FF = 16384

EPSILON = 1e-30
DECAY = 1.0 - 100.0 ** (-0.8)

ROWS_IN, COLS_IN = 64, 4096
ROWS_OUT, COLS_OUT = 256, 1024
HALF_IN, HALF_OUT = COLS_IN // 2, COLS_OUT // 2
PACK = (128, 2048)
BLOCKS = ROWS_OUT // 64
TILES_IN = HALF_IN // 128
TILES_OUT = HALF_OUT // 128

F32 = jnp.float32
VMEM = pl.BlockSpec(memory_space=pltpu.VMEM)
HBM = pl.BlockSpec(memory_space=pltpu.HBM)
PARAMS = pltpu.CompilerParams(vmem_limit_bytes=16 * 1024 * 1024)


def lanes(tile):
    return pl.ds(tile * 128, 128)


def widen_in(packed, block):
    packed[0:64, :] = block[...].astype(F32)


def widen_out(packed, block):
    for k in range(BLOCKS):
        packed[64:128, pl.ds(k * HALF_OUT, HALF_OUT)] = block[pl.ds(64 * k, 64), :].astype(F32)


def fetch_kernel(
    grad_in, grad_out, rows_in, rows_out, cols_in, cols_out,
    other, own_in, own_out, rows_in_here, rows_out_here, cols_in_here, cols_out_here,
    other_in, other_out, sems,
):
    own_half = lax.axis_index("dp")

    def block_in(half):
        return grad_in.at[:, pl.ds(pl.multiple_of(half * HALF_IN, 128), HALF_IN)]

    def block_out(half):
        return grad_out.at[:, pl.ds(pl.multiple_of(half * HALF_OUT, 128), HALF_OUT)]

    pairs = (
        (block_in(1 - own_half), other_in),
        (block_out(1 - own_half), other_out),
        (block_in(own_half), own_in),
        (block_out(own_half), own_out),
        (rows_in, rows_in_here),
        (rows_out, rows_out_here),
        (cols_in, cols_in_here),
        (cols_out, cols_out_here),
    )
    copies = [pltpu.make_async_copy(src, dst, sems.at[at]) for at, (src, dst) in enumerate(pairs)]
    for copy in copies:
        copy.start()
    copies[0].wait()
    widen_in(other, other_in)
    copies[1].wait()
    widen_out(other, other_out)
    for copy in copies[2:]:
        copy.wait()


def fetch(grad_in, grad_out, rows_in, rows_out, cols_in, cols_out):
    return pl.pallas_call(
        fetch_kernel,
        out_shape=(
            jax.ShapeDtypeStruct(PACK, F32),
            jax.ShapeDtypeStruct((ROWS_IN, HALF_IN), jnp.bfloat16),
            jax.ShapeDtypeStruct((ROWS_OUT, HALF_OUT), jnp.bfloat16),
        )
        + tuple(jax.ShapeDtypeStruct(x.shape, F32) for x in (rows_in, rows_out, cols_in, cols_out)),
        in_specs=[HBM] * 6,
        out_specs=(VMEM,) * 7,
        scratch_shapes=[
            pltpu.VMEM((ROWS_IN, HALF_IN), jnp.bfloat16),
            pltpu.VMEM((ROWS_OUT, HALF_OUT), jnp.bfloat16),
            pltpu.SemaphoreType.DMA((8,)),
        ],
        compiler_params=PARAMS,
        name="fetch",
    )(grad_in, grad_out, rows_in, rows_out, cols_in, cols_out)


def widen_kernel(own_in, own_out, packed):
    widen_in(packed, own_in)
    widen_out(packed, own_out)


def widen_own(own_in, own_out):
    return pl.pallas_call(
        widen_kernel,
        out_shape=jax.ShapeDtypeStruct(PACK, F32),
        in_specs=[VMEM, VMEM],
        out_specs=VMEM,
        compiler_params=PARAMS,
        name="widen_own",
    )(own_in, own_out)


def add_kernel(grad_in, grad_out, received, total, other_in, other_out, sems):
    half = 1 - lax.axis_index("dp")
    copy_in = pltpu.make_async_copy(
        grad_in.at[:, pl.ds(pl.multiple_of(half * HALF_IN, 128), HALF_IN)], other_in, sems.at[0]
    )
    copy_out = pltpu.make_async_copy(
        grad_out.at[:, pl.ds(pl.multiple_of(half * HALF_OUT, 128), HALF_OUT)], other_out, sems.at[1]
    )
    copy_in.start()
    copy_out.start()
    copy_in.wait()
    total[0:64, :] = received[0:64, :] + other_in[...].astype(F32)
    copy_out.wait()
    for k in range(BLOCKS):
        block = pl.ds(k * HALF_OUT, HALF_OUT)
        total[64:128, block] = received[64:128, block] + other_out[pl.ds(64 * k, 64), :].astype(F32)


def add_other(grad_in, grad_out, received):
    return pl.pallas_call(
        add_kernel,
        out_shape=jax.ShapeDtypeStruct(PACK, F32),
        in_specs=[HBM, HBM, VMEM],
        out_specs=VMEM,
        scratch_shapes=[
            pltpu.VMEM((ROWS_IN, HALF_IN), jnp.bfloat16),
            pltpu.VMEM((ROWS_OUT, HALF_OUT), jnp.bfloat16),
            pltpu.SemaphoreType.DMA((2,)),
        ],
        input_output_aliases={2: 0},
        cost_estimate=pl.CostEstimate(flops=262144, bytes_accessed=3 * 1024 * 1024, transcendentals=0),
        compiler_params=pltpu.CompilerParams(vmem_limit_bytes=4 * 1024 * 1024),
        name="add_other",
    )(grad_in, grad_out, received)


def rows_kernel(own, received, summed, row_sums):
    def lane_partial(row, tiles):
        total = None
        for tile in tiles:
            value = own[pl.ds(row, 64), lanes(tile)] + received[pl.ds(row, 64), lanes(tile)]
            summed[pl.ds(row, 64), lanes(tile)] = value
            square = value * value
            total = square if total is None else total + square
        return total

    def to_lanes(upper, lower):
        return jnp.sum(jnp.concatenate([upper, lower], axis=0).T, axis=0, keepdims=True)

    part = lane_partial(0, range(TILES_IN))
    vectors = [to_lanes(part, jnp.zeros_like(part))]
    for pair in range(BLOCKS // 2):
        upper, lower = (
            lane_partial(64, range(k * TILES_OUT, (k + 1) * TILES_OUT)) for k in (2 * pair, 2 * pair + 1)
        )
        vectors.append(to_lanes(upper, lower))
    for at, vector in enumerate(vectors):
        for peer in range(8):
            row_sums[peer, :, lanes(at)] = vector


def row_sums_of(own, received):
    return pl.pallas_call(
        rows_kernel,
        out_shape=(jax.ShapeDtypeStruct(PACK, F32), jax.ShapeDtypeStruct((8, 1, 384), F32)),
        in_specs=[VMEM, VMEM],
        out_specs=(VMEM, VMEM),
        compiler_params=PARAMS,
        name="row_sums",
    )(own, received)


def columns_kernel(row_sums, rows_in, rows_out, summed, scaled, row_scale, new_in, new_out, sends):
    total = jnp.sum(row_sums[...], axis=0)
    fresh_in = DECAY * rows_in[...] + (1.0 - DECAY) * (total[:, 0:64] * (1.0 / FF) + EPSILON)
    fresh_out = DECAY * rows_out[...] + (1.0 - DECAY) * (total[:, 128:384] * (1.0 / D) + EPSILON)
    new_in[...] = fresh_in
    new_out[...] = fresh_out
    root_in = lax.rsqrt(fresh_in)
    root_out = lax.rsqrt(fresh_out)

    def to_rows(vector):
        return jnp.broadcast_to(vector, (128, 128)).T

    row_scale[0:64, :] = to_rows(jnp.concatenate([root_in, root_in], axis=1))[0:64, :]
    row_scale[64:192, :] = to_rows(root_out[:, 0:128])
    row_scale[192:320, :] = to_rows(root_out[:, 128:256])

    def column(row, scale_row, tile):
        value = summed[pl.ds(row, 64), lanes(tile)]
        weighted = value * row_scale[pl.ds(scale_row, 64), :]
        scaled[pl.ds(row, 64), lanes(tile)] = weighted
        return (
            jnp.sum((value * value).reshape(8, 8, 128), axis=0),
            jnp.sum((weighted * weighted).reshape(8, 8, 128), axis=0),
        )

    def fold(value):
        return jnp.sum(value, axis=0, keepdims=True)

    def send(chunk, at, vector):
        for peer in range(8):
            sends[chunk * 8 + peer, :, lanes(at)] = vector

    for tile in range(TILES_IN):
        plain, weighted = column(0, 0, tile)
        send(tile // 2, tile % 2, fold(plain))
        send(tile // 2, 2 + tile % 2, fold(weighted))
    lane = lax.broadcasted_iota(jnp.int32, (1, 128), 1)
    for tile in range(TILES_OUT):
        plain, weighted = column(64, 64, tile)
        for k in range(1, BLOCKS):
            more = column(64, 64 + 64 * k, k * TILES_OUT + tile)
            plain, weighted = plain + more[0], weighted + more[1]
        plain, weighted = fold(plain), fold(weighted)
        send(2 * tile, 4, jnp.where(lane < 64, plain, pltpu.roll(weighted, 64, 1)))
        send(2 * tile + 1, 4, jnp.where(lane < 64, pltpu.roll(plain, 64, 1), weighted))


def column_sums_of(row_sums, rows_in, rows_out, summed):
    return pl.pallas_call(
        columns_kernel,
        out_shape=(
            jax.ShapeDtypeStruct(PACK, F32),
            jax.ShapeDtypeStruct((320, 128), F32),
            jax.ShapeDtypeStruct((1, ROWS_IN), F32),
            jax.ShapeDtypeStruct((1, ROWS_OUT), F32),
            jax.ShapeDtypeStruct((64, 1, 640), F32),
        ),
        in_specs=[VMEM] * 4,
        out_specs=(VMEM,) * 5,
        compiler_params=PARAMS,
        name="column_sums",
    )(row_sums, rows_in, rows_out, summed)


def factors_kernel(sums, cols_in, cols_out, sends):
    owner = lax.axis_index("dp") * 8 + lax.axis_index("z")
    total = jnp.sum(sums[...], axis=0)
    lane = lax.broadcasted_iota(jnp.int32, (1, 128), 1)
    new_in = DECAY * cols_in[owner] + (1.0 - DECAY) * (total[:, 0:256] * (1.0 / D) + EPSILON)
    energy_in = jnp.sum(total[:, 256:512] / new_in, axis=1, keepdims=True)
    mixed = total[:, 512:640]
    old_out = cols_out[owner // 2]
    old_out = jnp.where(owner % 2 == 1, pltpu.roll(old_out, 64, 1), old_out)
    new_out = DECAY * old_out + (1.0 - DECAY) * (mixed * (1.0 / FF) + EPSILON)
    weighted = jnp.where(lane < 64, pltpu.roll(mixed, 64, 1) / new_out, 0.0)
    energy_out = jnp.sum(weighted, axis=1, keepdims=True)
    last = jnp.where(lane < 64, new_out, jnp.where(lane < 96, energy_in, energy_out))
    for peer in range(64):
        sends[peer, :, 0:256] = new_in
        sends[peer, :, 256:384] = last


def factors_of(sums, cols_in, cols_out):
    return pl.pallas_call(
        factors_kernel,
        out_shape=jax.ShapeDtypeStruct((64, 1, 384), F32),
        in_specs=[VMEM] * 3,
        out_specs=VMEM,
        compiler_params=PARAMS,
        name="column_factors",
    )(sums, cols_in, cols_out)


def update_kernel(
    factors, scaled, row_scale, other, rows_in_new, rows_out_new,
    update_in, update_out, rows_in, rows_out, cols_in, cols_out,
    buf_in, buf_out, buf_cols, sems,
):
    own_half = lax.axis_index("dp")
    my_x = lax.axis_index("x")
    lane = lax.broadcasted_iota(jnp.int32, (1, 128), 1)
    copies = []

    def write(source, target):
        copy = pltpu.make_async_copy(source, target, sems.at[len(copies)])
        copy.start()
        copies.append(copy)

    write(rows_in_new, rows_in)
    write(rows_out_new, rows_out)
    energies = jnp.sum(factors[:, :, 256:384], axis=0)

    def limit(at):
        energy = jnp.sum(jnp.where(lane == at, energies, 0.0), axis=1, keepdims=True)
        return 1.0 / jnp.maximum(1.0, jnp.sqrt(energy * (1.0 / (D * FF))))

    limit_in, limit_out = limit(64), limit(96)

    def factor_in(half, tile):
        return factors[(half * 8 + tile // 2) * 4 + my_x, :, lanes(tile % 2)]

    def factor_out(half, tile):
        left = factors[(half * 8 + 2 * tile) * 4 + my_x, :, lanes(2)]
        right = factors[(half * 8 + 2 * tile + 1) * 4 + my_x, :, lanes(2)]
        return jnp.where(lane < 64, left, pltpu.roll(right, 64, 1))

    def block(buffer, target, offset, width, start):
        write(
            buffer.at[:, pl.ds(start, width)],
            target.at[:, pl.ds(pl.multiple_of(offset + start, 128), width)],
        )

    for which, half, source in ((0, own_half, scaled), (1, 1 - own_half, other)):

        def value(row, scale_row, tile):
            rows = source[pl.ds(row, 64), lanes(tile)]
            return rows if which == 0 else rows * row_scale[pl.ds(scale_row, 64), :]

        for tile in range(TILES_IN):
            factor = factor_in(half, tile)
            buf_cols[pl.ds(half * TILES_IN + tile, 1), :] = factor
            buf_in[which, :, lanes(tile)] = value(0, 0, tile) * (lax.rsqrt(factor) * limit_in)
            if tile % 4 == 3:
                block(buf_in.at[which], update_in, half * HALF_IN, 512, (tile - 3) * 128)
        for tile in range(TILES_OUT):
            factor = factor_out(half, tile)
            buf_cols[pl.ds(32 + half * TILES_OUT + tile, 1), :] = factor
            scale = lax.rsqrt(factor) * limit_out
            for k in range(BLOCKS):
                buf_out[which, pl.ds(64 * k, 64), lanes(tile)] = (
                    value(64, 64 + 64 * k, k * TILES_OUT + tile) * scale
                )
            if tile % 2 == 1:
                block(buf_out.at[which], update_out, half * HALF_OUT, 256, (tile - 1) * 128)
    write(buf_cols.at[0:32, :], cols_in)
    write(buf_cols.at[32:40, :], cols_out)
    for copy in copies:
        copy.wait()


def update_of(factors, scaled, row_scale, other, rows_in_new, rows_out_new):
    return pl.pallas_call(
        update_kernel,
        out_shape=(
            jax.ShapeDtypeStruct((ROWS_IN, COLS_IN), F32),
            jax.ShapeDtypeStruct((ROWS_OUT, COLS_OUT), F32),
            jax.ShapeDtypeStruct((1, ROWS_IN), F32),
            jax.ShapeDtypeStruct((1, ROWS_OUT), F32),
            jax.ShapeDtypeStruct((COLS_IN // 128, 128), F32),
            jax.ShapeDtypeStruct((COLS_OUT // 128, 128), F32),
        ),
        in_specs=[VMEM] * 6,
        out_specs=(HBM,) * 6,
        scratch_shapes=[
            pltpu.VMEM((2, ROWS_IN, HALF_IN), F32),
            pltpu.VMEM((2, ROWS_OUT, HALF_OUT), F32),
            pltpu.VMEM((40, 128), F32),
            pltpu.SemaphoreType.DMA((16,)),
        ],
        compiler_params=PARAMS,
        name="update",
    )(factors, scaled, row_scale, other, rows_in_new, rows_out_new)


def keep_in_hbm(x):
    return pltpu.with_memory_space_constraint(x, pltpu.HBM)


def per_device(grad_in, grad_out, rows_in, cols_in, rows_out, cols_out):
    swap = [(0, 1), (1, 0)]
    grad_in, grad_out = keep_in_hbm(grad_in[0]), keep_in_hbm(grad_out[0])
    first, own_in, own_out, rows_in, rows_out, cols_in, cols_out = fetch(
        grad_in,
        grad_out,
        keep_in_hbm(rows_in.reshape(1, ROWS_IN)),
        keep_in_hbm(rows_out.reshape(1, ROWS_OUT)),
        keep_in_hbm(cols_in.reshape(16, 1, 256)),
        keep_in_hbm(cols_out.reshape(8, 1, 128)),
    )
    arrived_own = lax.ppermute(first, "dp", swap)
    own = widen_own(own_in, own_out)
    arrived_other = lax.ppermute(own, "dp", swap)

    summed, row_sums = row_sums_of(own, arrived_own)
    row_sums = lax.all_to_all(row_sums, ("dp", "x"), 0, 0)
    other = add_other(grad_in, grad_out, arrived_other)
    scaled, row_scale, new_rows_in, new_rows_out, sums = column_sums_of(row_sums, rows_in, rows_out, summed)
    sums = lax.all_to_all(sums, ("z", "y"), 0, 0)
    factors = lax.all_to_all(factors_of(sums, cols_in, cols_out), ("dp", "z", "x"), 0, 0)
    update_in, update_out, new_rows_in, new_rows_out, new_cols_in, new_cols_out = update_of(
        factors, scaled, row_scale, other, new_rows_in, new_rows_out
    )
    return (
        update_in,
        update_out,
        new_rows_in.reshape(ROWS_IN),
        new_cols_in.reshape(COLS_IN),
        new_rows_out.reshape(ROWS_OUT),
        new_cols_out.reshape(COLS_OUT),
    )


def solution(mesh):
    fine = Mesh(mesh.devices.reshape(2, 8, 8, 4), ("dp", "z", "y", "x"))
    row = ("z", "y")
    return jax.shard_map(
        per_device,
        mesh=fine,
        in_specs=(
            P("dp", row, "x"),
            P("dp", row, "x"),
            P(row),
            P("x"),
            P(row),
            P("x"),
        ),
        out_specs=(P(row, "x"), P(row, "x"), P(row), P("x"), P(row), P("x")),
        check_vma=False,
    )
```

```python
import jax
import jax.numpy as jnp
from jax import lax
from jax.experimental import pallas as pl
from jax.experimental.pallas import tpu as pltpu
from jax.sharding import Mesh, PartitionSpec as P

D = 4096
FF = 16384

EPSILON = 1e-30
DECAY = 1.0 - 100.0 ** (-0.8)

ROWS_IN, COLS_IN = 64, 4096
ROWS_OUT, COLS_OUT = 256, 1024
HALF_IN, HALF_OUT = COLS_IN // 2, COLS_OUT // 2
PACK = (128, 2048)
BLOCKS = ROWS_OUT // 64
TILES_IN = HALF_IN // 128
TILES_OUT = HALF_OUT // 128

F32 = jnp.float32
VMEM = pl.BlockSpec(memory_space=pltpu.VMEM)
HBM = pl.BlockSpec(memory_space=pltpu.HBM)
ANY = pl.BlockSpec(memory_space=pl.ANY)
PARAMS = pltpu.CompilerParams(vmem_limit_bytes=16 * 1024 * 1024)


def lanes(tile):
    return pl.ds(tile * 128, 128)


def widen_in(packed, block):
    packed[0:64, :] = block[...].astype(F32)


def widen_out(packed, block):
    for k in range(BLOCKS):
        packed[64:128, pl.ds(k * HALF_OUT, HALF_OUT)] = block[pl.ds(64 * k, 64), :].astype(F32)


def fetch_kernel(
    grad_in, grad_out, rows_in, rows_out, cols_in, cols_out,
    other, own_in, own_out, rows_in_here, rows_out_here, cols_in_here, cols_out_here,
    other_in, other_out, sems,
):
    own_half = lax.axis_index("dp")

    def block_in(half):
        return grad_in.at[:, pl.ds(pl.multiple_of(half * HALF_IN, 128), HALF_IN)]

    def block_out(half):
        return grad_out.at[:, pl.ds(pl.multiple_of(half * HALF_OUT, 128), HALF_OUT)]

    pairs = (
        (block_in(1 - own_half), other_in),
        (block_out(1 - own_half), other_out),
        (block_in(own_half), own_in),
        (block_out(own_half), own_out),
        (rows_in, rows_in_here),
        (rows_out, rows_out_here),
        (cols_in, cols_in_here),
        (cols_out, cols_out_here),
    )
    copies = [pltpu.make_async_copy(src, dst, sems.at[at]) for at, (src, dst) in enumerate(pairs)]
    for copy in copies:
        copy.start()
    copies[0].wait()
    widen_in(other, other_in)
    copies[1].wait()
    widen_out(other, other_out)
    for copy in copies[2:]:
        copy.wait()


def fetch(grad_in, grad_out, rows_in, rows_out, cols_in, cols_out):
    return pl.pallas_call(
        fetch_kernel,
        out_shape=(
            jax.ShapeDtypeStruct(PACK, F32),
            jax.ShapeDtypeStruct((ROWS_IN, HALF_IN), jnp.bfloat16),
            jax.ShapeDtypeStruct((ROWS_OUT, HALF_OUT), jnp.bfloat16),
        )
        + tuple(jax.ShapeDtypeStruct(x.shape, F32) for x in (rows_in, rows_out, cols_in, cols_out)),
        in_specs=[HBM] * 6,
        out_specs=(VMEM,) * 7,
        scratch_shapes=[
            pltpu.VMEM((ROWS_IN, HALF_IN), jnp.bfloat16),
            pltpu.VMEM((ROWS_OUT, HALF_OUT), jnp.bfloat16),
            pltpu.SemaphoreType.DMA((8,)),
        ],
        compiler_params=PARAMS,
        name="fetch",
    )(grad_in, grad_out, rows_in, rows_out, cols_in, cols_out)


def widen_kernel(own_in, own_out, packed):
    widen_in(packed, own_in)
    widen_out(packed, own_out)


def widen_own(own_in, own_out):
    return pl.pallas_call(
        widen_kernel,
        out_shape=jax.ShapeDtypeStruct(PACK, F32),
        in_specs=[VMEM, VMEM],
        out_specs=VMEM,
        compiler_params=PARAMS,
        name="widen_own",
    )(own_in, own_out)


def add_kernel(grad_in, grad_out, received, total, other_in, other_out, sems):
    half = 1 - lax.axis_index("dp")
    copy_in = pltpu.make_async_copy(
        grad_in.at[:, pl.ds(pl.multiple_of(half * HALF_IN, 128), HALF_IN)], other_in, sems.at[0]
    )
    copy_out = pltpu.make_async_copy(
        grad_out.at[:, pl.ds(pl.multiple_of(half * HALF_OUT, 128), HALF_OUT)], other_out, sems.at[1]
    )
    copy_in.start()
    copy_out.start()
    copy_in.wait()
    total[0:64, :] = received[0:64, :] + other_in[...].astype(F32)
    copy_out.wait()
    for k in range(BLOCKS):
        block = pl.ds(k * HALF_OUT, HALF_OUT)
        total[64:128, block] = received[64:128, block] + other_out[pl.ds(64 * k, 64), :].astype(F32)


def add_other(grad_in, grad_out, received):
    return pl.pallas_call(
        add_kernel,
        out_shape=jax.ShapeDtypeStruct(PACK, F32),
        in_specs=[HBM, HBM, VMEM],
        out_specs=VMEM,
        scratch_shapes=[
            pltpu.VMEM((ROWS_IN, HALF_IN), jnp.bfloat16),
            pltpu.VMEM((ROWS_OUT, HALF_OUT), jnp.bfloat16),
            pltpu.SemaphoreType.DMA((2,)),
        ],
        input_output_aliases={2: 0},
        cost_estimate=pl.CostEstimate(flops=262144, bytes_accessed=3 * 1024 * 1024, transcendentals=0),
        compiler_params=pltpu.CompilerParams(vmem_limit_bytes=4 * 1024 * 1024),
        name="add_other",
    )(grad_in, grad_out, received)


def rows_kernel(own, received, summed, row_sums):
    def lane_partial(row, tiles):
        total = None
        for tile in tiles:
            value = own[pl.ds(row, 64), lanes(tile)] + received[pl.ds(row, 64), lanes(tile)]
            summed[pl.ds(row, 64), lanes(tile)] = value
            square = value * value
            total = square if total is None else total + square
        return total

    def to_lanes(upper, lower):
        return jnp.sum(jnp.concatenate([upper, lower], axis=0).T, axis=0, keepdims=True)

    part = lane_partial(0, range(TILES_IN))
    vectors = [to_lanes(part, jnp.zeros_like(part))]
    for pair in range(BLOCKS // 2):
        upper, lower = (
            lane_partial(64, range(k * TILES_OUT, (k + 1) * TILES_OUT)) for k in (2 * pair, 2 * pair + 1)
        )
        vectors.append(to_lanes(upper, lower))
    for at, vector in enumerate(vectors):
        for peer in range(8):
            row_sums[peer, :, lanes(at)] = vector


def row_sums_of(own, received):
    return pl.pallas_call(
        rows_kernel,
        out_shape=(jax.ShapeDtypeStruct(PACK, F32), jax.ShapeDtypeStruct((8, 1, 384), F32)),
        in_specs=[VMEM, VMEM],
        out_specs=(VMEM, VMEM),
        compiler_params=PARAMS,
        name="row_sums",
    )(own, received)


def columns_kernel(
    row_sums, rows_in, rows_out, summed, other, scaled, row_scale, new_in, new_out, sends, other_on
):
    del other, other_on
    total = jnp.sum(row_sums[...], axis=0)
    fresh_in = DECAY * rows_in[...] + (1.0 - DECAY) * (total[:, 0:64] * (1.0 / FF) + EPSILON)
    fresh_out = DECAY * rows_out[...] + (1.0 - DECAY) * (total[:, 128:384] * (1.0 / D) + EPSILON)
    new_in[...] = fresh_in
    new_out[...] = fresh_out
    root_in = lax.rsqrt(fresh_in)
    root_out = lax.rsqrt(fresh_out)

    def to_rows(vector):
        return jnp.broadcast_to(vector, (128, 128)).T

    row_scale[0:64, :] = to_rows(jnp.concatenate([root_in, root_in], axis=1))[0:64, :]
    row_scale[64:192, :] = to_rows(root_out[:, 0:128])
    row_scale[192:320, :] = to_rows(root_out[:, 128:256])

    def column(row, scale_row, tile):
        value = summed[pl.ds(row, 64), lanes(tile)]
        weighted = value * row_scale[pl.ds(scale_row, 64), :]
        scaled[pl.ds(row, 64), lanes(tile)] = weighted
        return (
            jnp.sum((value * value).reshape(8, 8, 128), axis=0),
            jnp.sum((weighted * weighted).reshape(8, 8, 128), axis=0),
        )

    def fold(value):
        return jnp.sum(value, axis=0, keepdims=True)

    def send(chunk, row, vector):
        for peer in range(chunk, 8, 2):
            sends[peer, pl.ds(row, 1), :] = vector

    for tile in range(TILES_IN):
        plain, weighted = column(0, 0, tile)
        send(tile // 8, tile % 8, fold(plain))
        send(tile // 8, 8 + tile % 8, fold(weighted))
    for tile in range(TILES_OUT):
        plain, weighted = column(64, 64, tile)
        for k in range(1, BLOCKS):
            more = column(64, 64 + 64 * k, k * TILES_OUT + tile)
            plain, weighted = plain + more[0], weighted + more[1]
        send(tile // 2, 16 + tile % 2, fold(plain))
        send(tile // 2, 18 + tile % 2, fold(weighted))
    for peer in range(8):
        sends[peer, 20:24, :] = jnp.zeros((4, 128), F32)


def column_sums_of(row_sums, rows_in, rows_out, summed, other):
    return pl.pallas_call(
        columns_kernel,
        out_shape=(
            jax.ShapeDtypeStruct(PACK, F32),
            jax.ShapeDtypeStruct((320, 128), F32),
            jax.ShapeDtypeStruct((1, ROWS_IN), F32),
            jax.ShapeDtypeStruct((1, ROWS_OUT), F32),
            jax.ShapeDtypeStruct((8, 24, 128), F32),
            jax.ShapeDtypeStruct(PACK, F32),
        ),
        in_specs=[VMEM] * 4 + [ANY],
        out_specs=(VMEM,) * 5 + (ANY,),
        input_output_aliases={4: 5},
        compiler_params=PARAMS,
        name="column_sums",
    )(row_sums, rows_in, rows_out, summed, other)


def total_kernel(sums, sends):
    total = sums[0]
    for peer in range(1, 8):
        total = total + sums[peer]
    for peer in range(8):
        sends[peer] = total


def total_of(sums):
    return pl.pallas_call(
        total_kernel,
        out_shape=jax.ShapeDtypeStruct((8, 24, 128), F32),
        in_specs=[VMEM],
        out_specs=VMEM,
        compiler_params=PARAMS,
        name="total",
    )(sums)


def factors_kernel(sums, cols_in, cols_out, sends):
    chunk = lax.axis_index("dp") * 2 + lax.axis_index("pair")
    total = sums[0]
    for peer in range(1, 8):
        total = total + sums[peer]
    new_in = DECAY * cols_in[chunk] + (1.0 - DECAY) * (total[0:8] * (1.0 / D) + EPSILON)
    new_out = DECAY * cols_out[chunk] + (1.0 - DECAY) * (total[16:18] * (1.0 / FF) + EPSILON)
    energy_in = jnp.sum(total[8:16] / new_in, axis=0, keepdims=True)
    energy_out = jnp.sum(total[18:20] / new_out, axis=0, keepdims=True)
    for peer in range(16):
        sends[peer, 0:8, :] = new_in
        sends[peer, 8:10, :] = new_out
        sends[peer, 10:11, :] = energy_in
        sends[peer, 11:12, :] = energy_out
        sends[peer, 12:16, :] = jnp.zeros((4, 128), F32)


def factors_of(sums, cols_in, cols_out):
    return pl.pallas_call(
        factors_kernel,
        out_shape=jax.ShapeDtypeStruct((16, 16, 128), F32),
        in_specs=[VMEM] * 3,
        out_specs=VMEM,
        compiler_params=PARAMS,
        name="column_factors",
    )(sums, cols_in, cols_out)


def update_kernel(
    factors, scaled, row_scale, other, rows_in_new, rows_out_new,
    update_in, update_out, rows_in, rows_out, cols_in, cols_out,
    buf_in, buf_out, buf_cols, sems,
):
    own_half = lax.axis_index("dp")
    my_x = lax.axis_index("x")
    copies = []

    def write(source, target):
        copy = pltpu.make_async_copy(source, target, sems.at[len(copies)])
        copy.start()
        copies.append(copy)

    write(rows_in_new, rows_in)
    write(rows_out_new, rows_out)

    def limit(row):
        parts = factors[0, row : row + 1, :]
        for peer in range(1, 16):
            parts = parts + factors[peer, row : row + 1, :]
        energy = jnp.sum(parts, axis=1, keepdims=True)
        return 1.0 / jnp.maximum(1.0, jnp.sqrt(energy * (1.0 / (D * FF))))

    limit_in, limit_out = limit(10), limit(11)

    def factor_in(half, tile):
        return factors[(half * 2 + tile // 8) * 4 + my_x, pl.ds(tile % 8, 1), :]

    def factor_out(half, tile):
        return factors[(half * 2 + tile // 2) * 4 + my_x, pl.ds(8 + tile % 2, 1), :]

    def block(buffer, target, offset, width, start):
        write(
            buffer.at[:, pl.ds(start, width)],
            target.at[:, pl.ds(pl.multiple_of(offset + start, 128), width)],
        )

    for which, half, source in ((0, own_half, scaled), (1, 1 - own_half, other)):

        def value(row, scale_row, tile):
            rows = source[pl.ds(row, 64), lanes(tile)]
            return rows if which == 0 else rows * row_scale[pl.ds(scale_row, 64), :]

        for tile in range(TILES_IN):
            factor = factor_in(half, tile)
            buf_cols[pl.ds(half * TILES_IN + tile, 1), :] = factor
            buf_in[which, :, lanes(tile)] = value(0, 0, tile) * (lax.rsqrt(factor) * limit_in)
            if tile % 4 == 3:
                block(buf_in.at[which], update_in, half * HALF_IN, 512, (tile - 3) * 128)
        for tile in range(TILES_OUT):
            factor = factor_out(half, tile)
            buf_cols[pl.ds(32 + half * TILES_OUT + tile, 1), :] = factor
            scale = lax.rsqrt(factor) * limit_out
            for k in range(BLOCKS):
                buf_out[which, pl.ds(64 * k, 64), lanes(tile)] = (
                    value(64, 64 + 64 * k, k * TILES_OUT + tile) * scale
                )
            if tile % 2 == 1:
                block(buf_out.at[which], update_out, half * HALF_OUT, 256, (tile - 1) * 128)
    write(buf_cols.at[0:32, :], cols_in)
    write(buf_cols.at[32:40, :], cols_out)
    for copy in copies:
        copy.wait()


def update_of(factors, scaled, row_scale, other, rows_in_new, rows_out_new):
    return pl.pallas_call(
        update_kernel,
        out_shape=(
            jax.ShapeDtypeStruct((ROWS_IN, COLS_IN), F32),
            jax.ShapeDtypeStruct((ROWS_OUT, COLS_OUT), F32),
            jax.ShapeDtypeStruct((1, ROWS_IN), F32),
            jax.ShapeDtypeStruct((1, ROWS_OUT), F32),
            jax.ShapeDtypeStruct((COLS_IN // 128, 128), F32),
            jax.ShapeDtypeStruct((COLS_OUT // 128, 128), F32),
        ),
        in_specs=[VMEM] * 6,
        out_specs=(HBM,) * 6,
        scratch_shapes=[
            pltpu.VMEM((2, ROWS_IN, HALF_IN), F32),
            pltpu.VMEM((2, ROWS_OUT, HALF_OUT), F32),
            pltpu.VMEM((40, 128), F32),
            pltpu.SemaphoreType.DMA((16,)),
        ],
        compiler_params=PARAMS,
        name="update",
    )(factors, scaled, row_scale, other, rows_in_new, rows_out_new)


def keep_in_hbm(x):
    return pltpu.with_memory_space_constraint(x, pltpu.HBM)


def per_device(grad_in, grad_out, rows_in, cols_in, rows_out, cols_out):
    swap = [(0, 1), (1, 0)]
    grad_in, grad_out = keep_in_hbm(grad_in[0]), keep_in_hbm(grad_out[0])
    first, own_in, own_out, rows_in, rows_out, cols_in, cols_out = fetch(
        grad_in,
        grad_out,
        keep_in_hbm(rows_in.reshape(1, ROWS_IN)),
        keep_in_hbm(rows_out.reshape(1, ROWS_OUT)),
        keep_in_hbm(cols_in.reshape(4, 8, 128)),
        keep_in_hbm(cols_out.reshape(4, 2, 128)),
    )
    arrived_own = lax.ppermute(first, "dp", swap)
    own = widen_own(own_in, own_out)
    arrived_other = lax.ppermute(own, "dp", swap)

    summed, row_sums = row_sums_of(own, arrived_own)
    row_sums = lax.all_to_all(row_sums, ("dp", "x"), 0, 0)
    other = add_other(grad_in, grad_out, arrived_other)
    scaled, row_scale, new_rows_in, new_rows_out, sums, other = column_sums_of(
        row_sums, rows_in, rows_out, summed, other
    )
    sums = lax.all_to_all(sums, ("y", "pair"), 0, 0)
    sums = lax.all_to_all(total_of(sums), "z", 0, 0)
    factors = lax.all_to_all(factors_of(sums, cols_in, cols_out), ("dp", "pair", "x"), 0, 0)
    update_in, update_out, new_rows_in, new_rows_out, new_cols_in, new_cols_out = update_of(
        factors, scaled, row_scale, other, new_rows_in, new_rows_out
    )
    return (
        update_in,
        update_out,
        new_rows_in.reshape(ROWS_IN),
        new_cols_in.reshape(COLS_IN),
        new_rows_out.reshape(ROWS_OUT),
        new_cols_out.reshape(COLS_OUT),
    )


def solution(mesh):
    fine = Mesh(mesh.devices.reshape(2, 8, 4, 2, 4), ("dp", "z", "y", "pair", "x"))
    row = ("z", "y", "pair")
    return jax.shard_map(
        per_device,
        mesh=fine,
        in_specs=(
            P("dp", row, "x"),
            P("dp", row, "x"),
            P(row),
            P("x"),
            P(row),
            P("x"),
        ),
        out_specs=(P(row, "x"), P(row, "x"), P(row), P("x"), P(row), P("x")),
        check_vma=False,
    )
```

```python
import jax
import jax.numpy as jnp
from jax import lax
from jax.experimental import pallas as pl
from jax.experimental.pallas import tpu as pltpu
from jax.sharding import Mesh, PartitionSpec as P

D = 4096
FF = 16384

EPSILON = 1e-30
DECAY = 1.0 - 100.0 ** (-0.8)

ROWS_IN, COLS_IN = 64, 4096
ROWS_OUT, COLS_OUT = 256, 1024
HALF_IN, HALF_OUT = COLS_IN // 2, COLS_OUT // 2
PACK = (128, 2048)
BLOCKS = ROWS_OUT // 64
TILES_IN = HALF_IN // 128
TILES_OUT = HALF_OUT // 128

F32 = jnp.float32
VMEM = pl.BlockSpec(memory_space=pltpu.VMEM)
HBM = pl.BlockSpec(memory_space=pltpu.HBM)
ANY = pl.BlockSpec(memory_space=pl.ANY)
PARAMS = pltpu.CompilerParams(vmem_limit_bytes=16 * 1024 * 1024)


def lanes(tile):
    return pl.ds(tile * 128, 128)


def half_copies(grad_in, grad_out, half, block_in, block_out, sems):
    columns_in = pl.ds(pl.multiple_of(half * HALF_IN, 128), HALF_IN)
    columns_out = pl.ds(pl.multiple_of(half * HALF_OUT, 128), HALF_OUT)
    return (
        pltpu.make_async_copy(grad_in.at[:, columns_in], block_in, sems.at[0]),
        pltpu.make_async_copy(grad_out.at[:, columns_out], block_out, sems.at[1]),
    )


HALF_SCRATCH = [
    pltpu.VMEM((ROWS_IN, HALF_IN), jnp.bfloat16),
    pltpu.VMEM((ROWS_OUT, HALF_OUT), jnp.bfloat16),
]


def fetch_kernel(grad_in, grad_out, other, other_in, other_out, sems):
    copies = half_copies(grad_in, grad_out, 1 - lax.axis_index("dp"), other_in, other_out, sems)
    for copy in copies:
        copy.start()
    copies[0].wait()
    other[0:64, :] = other_in[...].astype(F32)
    copies[1].wait()
    for k in range(BLOCKS):
        other[64:128, pl.ds(k * HALF_OUT, HALF_OUT)] = other_out[pl.ds(64 * k, 64), :].astype(F32)


def fetch(grad_in, grad_out):
    return pl.pallas_call(
        fetch_kernel,
        out_shape=jax.ShapeDtypeStruct(PACK, F32),
        in_specs=[HBM, HBM],
        out_specs=VMEM,
        scratch_shapes=HALF_SCRATCH + [pltpu.SemaphoreType.DMA((2,))],
        compiler_params=PARAMS,
        name="fetch",
    )(grad_in, grad_out)


def widen_kernel(grad_in, grad_out, packed):
    half = lax.axis_index("dp")
    packed[0:64, :] = grad_in[:, pl.ds(pl.multiple_of(half * HALF_IN, 128), HALF_IN)].astype(F32)
    columns = pl.ds(pl.multiple_of(half * HALF_OUT, 128), HALF_OUT)
    for k in range(BLOCKS):
        packed[64:128, pl.ds(k * HALF_OUT, HALF_OUT)] = grad_out[pl.ds(64 * k, 64), columns].astype(F32)


def widen_own(grad_in, grad_out):
    return pl.pallas_call(
        widen_kernel,
        out_shape=jax.ShapeDtypeStruct(PACK, F32),
        in_specs=[VMEM, VMEM],
        out_specs=VMEM,
        compiler_params=PARAMS,
        name="widen_own",
    )(grad_in, grad_out)


def add_kernel(grad_in, grad_out, received, *refs):
    total, other_in, other_out, sems = refs[4], refs[9], refs[10], refs[11]
    copies = half_copies(grad_in, grad_out, 1 - lax.axis_index("dp"), other_in, other_out, sems)
    small = [pltpu.make_async_copy(refs[at], refs[5 + at], sems.at[2 + at]) for at in range(4)]
    for copy in (*copies, *small):
        copy.start()
    copies[0].wait()
    total[0:64, :] = received[0:64, :] + other_in[...].astype(F32)
    copies[1].wait()
    for k in range(BLOCKS):
        block = pl.ds(k * HALF_OUT, HALF_OUT)
        total[64:128, block] = received[64:128, block] + other_out[pl.ds(64 * k, 64), :].astype(F32)
    for copy in small:
        copy.wait()


def add_other(grad_in, grad_out, received, *factors):
    return pl.pallas_call(
        add_kernel,
        out_shape=tuple(jax.ShapeDtypeStruct(x.shape, F32) for x in (received, *factors)),
        in_specs=[HBM, HBM, VMEM] + [HBM] * 4,
        out_specs=(VMEM,) * 5,
        scratch_shapes=HALF_SCRATCH + [pltpu.SemaphoreType.DMA((6,))],
        input_output_aliases={2: 0},
        cost_estimate=pl.CostEstimate(flops=262144, bytes_accessed=3 * 1024 * 1024, transcendentals=0),
        compiler_params=pltpu.CompilerParams(vmem_limit_bytes=4 * 1024 * 1024),
        name="add_other",
    )(grad_in, grad_out, received, *factors)


def rows_kernel(own, received, summed, row_sums):
    def lane_partial(row, tiles):
        total = None
        for tile in tiles:
            value = own[pl.ds(row, 64), lanes(tile)] + received[pl.ds(row, 64), lanes(tile)]
            summed[pl.ds(row, 64), lanes(tile)] = value
            square = value * value
            total = square if total is None else total + square
        return total

    def to_lanes(upper, lower):
        return jnp.sum(jnp.concatenate([upper, lower], axis=0).T, axis=0, keepdims=True)

    part = lane_partial(0, range(TILES_IN))
    vectors = [to_lanes(part, jnp.zeros_like(part))]
    for pair in range(BLOCKS // 2):
        upper, lower = (
            lane_partial(64, range(k * TILES_OUT, (k + 1) * TILES_OUT)) for k in (2 * pair, 2 * pair + 1)
        )
        vectors.append(to_lanes(upper, lower))
    for at, vector in enumerate(vectors):
        for peer in range(8):
            row_sums[peer, :, lanes(at)] = vector


def row_sums_of(own, received):
    return pl.pallas_call(
        rows_kernel,
        out_shape=(jax.ShapeDtypeStruct(PACK, F32), jax.ShapeDtypeStruct((8, 1, 384), F32)),
        in_specs=[VMEM, VMEM],
        out_specs=(VMEM, VMEM),
        compiler_params=PARAMS,
        name="row_sums",
    )(own, received)


def columns_kernel(
    row_sums, rows_in, rows_out, summed, other, scaled, row_scale, new_in, new_out, sends, other_on
):
    del other, other_on
    total = jnp.sum(row_sums[...], axis=0)
    fresh_in = DECAY * rows_in[...] + (1.0 - DECAY) * (total[:, 0:64] * (1.0 / FF) + EPSILON)
    fresh_out = DECAY * rows_out[...] + (1.0 - DECAY) * (total[:, 128:384] * (1.0 / D) + EPSILON)
    new_in[...] = fresh_in
    new_out[...] = fresh_out
    root_in = lax.rsqrt(fresh_in)
    root_out = lax.rsqrt(fresh_out)

    def to_rows(vector):
        return jnp.broadcast_to(vector, (128, 128)).T

    row_scale[0:64, :] = to_rows(jnp.concatenate([root_in, root_in], axis=1))[0:64, :]
    row_scale[64:192, :] = to_rows(root_out[:, 0:128])
    row_scale[192:320, :] = to_rows(root_out[:, 128:256])

    def column(row, scale_row, tile):
        value = summed[pl.ds(row, 64), lanes(tile)]
        weighted = value * row_scale[pl.ds(scale_row, 64), :]
        scaled[pl.ds(row, 64), lanes(tile)] = weighted
        return (
            jnp.sum((value * value).reshape(8, 8, 128), axis=0),
            jnp.sum((weighted * weighted).reshape(8, 8, 128), axis=0),
        )

    def fold(value):
        return jnp.sum(value, axis=0, keepdims=True)

    def send(chunk, row, vector):
        for peer in range(chunk, 8, 2):
            sends[peer, row // 4, row % 4 : row % 4 + 1, :] = vector

    for tile in range(TILES_IN):
        plain, weighted = column(0, 0, tile)
        send(tile // 8, tile % 8, fold(plain))
        send(tile // 8, 8 + tile % 8, fold(weighted))
    for tile in range(TILES_OUT):
        plain, weighted = column(64, 64, tile)
        for k in range(1, BLOCKS):
            more = column(64, 64 + 64 * k, k * TILES_OUT + tile)
            plain, weighted = plain + more[0], weighted + more[1]
        send(tile // 2, 16 + tile % 2, fold(plain))
        send(tile // 2, 18 + tile % 2, fold(weighted))


def column_sums_of(row_sums, rows_in, rows_out, summed, other):
    return pl.pallas_call(
        columns_kernel,
        out_shape=(
            jax.ShapeDtypeStruct(PACK, F32),
            jax.ShapeDtypeStruct((320, 128), F32),
            jax.ShapeDtypeStruct((1, ROWS_IN), F32),
            jax.ShapeDtypeStruct((1, ROWS_OUT), F32),
            jax.ShapeDtypeStruct((8, 5, 4, 128), F32),
            jax.ShapeDtypeStruct(PACK, F32),
        ),
        in_specs=[VMEM] * 4 + [ANY],
        out_specs=(VMEM,) * 5 + (ANY,),
        input_output_aliases={4: 5},
        compiler_params=PARAMS,
        name="column_sums",
    )(row_sums, rows_in, rows_out, summed, other)


def total_kernel(sums, sends):
    total = sums[0]
    for peer in range(1, 8):
        total = total + sums[peer]
    for peer in range(8):
        sends[peer] = total


def total_of(sums):
    return pl.pallas_call(
        total_kernel,
        out_shape=jax.ShapeDtypeStruct((8, 5, 4, 128), F32),
        in_specs=[VMEM],
        out_specs=VMEM,
        compiler_params=PARAMS,
        name="total",
    )(sums)


def factors_kernel(sums, cols_in, cols_out, sends):
    chunk = lax.axis_index("dp") * 2 + lax.axis_index("pair")
    total = sums[0]
    for peer in range(1, 8):
        total = total + sums[peer]
    energy_in = jnp.zeros((1, 128), F32)
    for part in range(2):
        new_in = DECAY * cols_in[chunk * 2 + part] + (1.0 - DECAY) * (total[part] * (1.0 / D) + EPSILON)
        energy_in += jnp.sum(total[2 + part] / new_in, axis=0, keepdims=True)
        for peer in range(16):
            sends[peer, part] = new_in
    new_out = DECAY * cols_out[chunk] + (1.0 - DECAY) * (total[4, 0:2] * (1.0 / FF) + EPSILON)
    energy_out = jnp.sum(total[4, 2:4] / new_out, axis=0, keepdims=True)
    last = jnp.concatenate([new_out, energy_in, energy_out], axis=0)
    for peer in range(16):
        sends[peer, 2] = last


def factors_of(sums, cols_in, cols_out):
    return pl.pallas_call(
        factors_kernel,
        out_shape=jax.ShapeDtypeStruct((16, 3, 4, 128), F32),
        in_specs=[VMEM] * 3,
        out_specs=VMEM,
        compiler_params=PARAMS,
        name="column_factors",
    )(sums, cols_in, cols_out)


def update_kernel(
    factors, scaled, row_scale, other, rows_in_new, rows_out_new,
    update_in, update_out, rows_in, rows_out, cols_in, cols_out,
    buf_in, buf_out, buf_cols, sems,
):
    own_half = lax.axis_index("dp")
    my_x = lax.axis_index("x")
    copies = []

    def write(source, target):
        copy = pltpu.make_async_copy(source, target, sems.at[len(copies)])
        copy.start()
        copies.append(copy)


    energies = factors[0, 2]
    for peer in range(1, 16):
        energies = energies + factors[peer, 2]

    def limit(row):
        energy = jnp.sum(energies[row : row + 1, :], axis=1, keepdims=True)
        return 1.0 / jnp.maximum(1.0, jnp.sqrt(energy * (1.0 / (D * FF))))

    limit_in, limit_out = limit(2), limit(3)

    def factor_in(half, tile):
        return factors[(half * 2 + tile // 8) * 4 + my_x, tile // 4 % 2, pl.ds(tile % 4, 1), :]

    def factor_out(half, tile):
        return factors[(half * 2 + tile // 2) * 4 + my_x, 2, pl.ds(tile % 2, 1), :]

    def block(buffer, target, offset, width, start):
        write(
            buffer.at[:, pl.ds(start, width)],
            target.at[:, pl.ds(pl.multiple_of(offset + start, 128), width)],
        )

    for which, half, source in ((0, own_half, scaled), (1, 1 - own_half, other)):

        def value(row, scale_row, tile):
            rows = source[pl.ds(row, 64), lanes(tile)]
            return rows if which == 0 else rows * row_scale[pl.ds(scale_row, 64), :]

        for tile in range(TILES_IN):
            factor = factor_in(half, tile)
            buf_cols[pl.ds(half * TILES_IN + tile, 1), :] = factor
            buf_in[which, :, lanes(tile)] = value(0, 0, tile) * (lax.rsqrt(factor) * limit_in)
            if tile % 8 == 7:
                block(buf_in.at[which], update_in, half * HALF_IN, 1024, (tile - 7) * 128)
        for tile in range(TILES_OUT):
            factor = factor_out(half, tile)
            buf_cols[pl.ds(32 + half * TILES_OUT + tile, 1), :] = factor
            scale = lax.rsqrt(factor) * limit_out
            for k in range(BLOCKS):
                buf_out[which, pl.ds(64 * k, 64), lanes(tile)] = (
                    value(64, 64 + 64 * k, k * TILES_OUT + tile) * scale
                )
            if tile % 2 == 1:
                block(buf_out.at[which], update_out, half * HALF_OUT, 256, (tile - 1) * 128)
    write(rows_in_new, rows_in)
    write(rows_out_new, rows_out)
    write(buf_cols.at[0:32, :], cols_in)
    write(buf_cols.at[32:40, :], cols_out)
    for copy in copies:
        copy.wait()


def update_of(factors, scaled, row_scale, other, rows_in_new, rows_out_new):
    return pl.pallas_call(
        update_kernel,
        out_shape=(
            jax.ShapeDtypeStruct((ROWS_IN, COLS_IN), F32),
            jax.ShapeDtypeStruct((ROWS_OUT, COLS_OUT), F32),
            jax.ShapeDtypeStruct((1, ROWS_IN), F32),
            jax.ShapeDtypeStruct((1, ROWS_OUT), F32),
            jax.ShapeDtypeStruct((COLS_IN // 128, 128), F32),
            jax.ShapeDtypeStruct((COLS_OUT // 128, 128), F32),
        ),
        in_specs=[VMEM] * 6,
        out_specs=(HBM,) * 6,
        scratch_shapes=[
            pltpu.VMEM((2, ROWS_IN, HALF_IN), F32),
            pltpu.VMEM((2, ROWS_OUT, HALF_OUT), F32),
            pltpu.VMEM((40, 128), F32),
            pltpu.SemaphoreType.DMA((12,)),
        ],
        compiler_params=PARAMS,
        name="update",
    )(factors, scaled, row_scale, other, rows_in_new, rows_out_new)


def keep_in_hbm(x):
    return pltpu.with_memory_space_constraint(x, pltpu.HBM)


def per_device(grad_in, grad_out, rows_in, cols_in, rows_out, cols_out):
    swap = [(0, 1), (1, 0)]
    grad_in, grad_out = grad_in[0], grad_out[0]
    grad_in_far, grad_out_far = keep_in_hbm(grad_in), keep_in_hbm(grad_out)
    arrived_own = lax.ppermute(fetch(grad_in_far, grad_out_far), "dp", swap)
    own = widen_own(grad_in, grad_out)
    arrived_other = lax.ppermute(own, "dp", swap)

    summed, row_sums = row_sums_of(own, arrived_own)
    row_sums = lax.all_to_all(row_sums, ("dp", "x"), 0, 0)
    other, rows_in, rows_out, cols_in, cols_out = add_other(
        grad_in_far,
        grad_out_far,
        arrived_other,
        keep_in_hbm(rows_in.reshape(1, ROWS_IN)),
        keep_in_hbm(rows_out.reshape(1, ROWS_OUT)),
        keep_in_hbm(cols_in.reshape(8, 4, 128)),
        keep_in_hbm(cols_out.reshape(4, 2, 128)),
    )
    scaled, row_scale, new_rows_in, new_rows_out, sums, other = column_sums_of(
        row_sums, rows_in, rows_out, summed, other
    )
    sums = lax.all_to_all(sums, ("y", "pair"), 0, 0)
    sums = lax.all_to_all(total_of(sums), "z", 0, 0)
    factors = lax.all_to_all(factors_of(sums, cols_in, cols_out), ("dp", "pair", "x"), 0, 0)
    update_in, update_out, new_rows_in, new_rows_out, new_cols_in, new_cols_out = update_of(
        factors, scaled, row_scale, other, new_rows_in, new_rows_out
    )
    return (
        update_in,
        update_out,
        new_rows_in.reshape(ROWS_IN),
        new_cols_in.reshape(COLS_IN),
        new_rows_out.reshape(ROWS_OUT),
        new_cols_out.reshape(COLS_OUT),
    )


def solution(mesh):
    fine = Mesh(mesh.devices.reshape(2, 8, 4, 2, 4), ("dp", "z", "y", "pair", "x"))
    row = ("z", "y", "pair")
    return jax.shard_map(
        per_device,
        mesh=fine,
        in_specs=(
            P("dp", row, "x"),
            P("dp", row, "x"),
            P(row),
            P("x"),
            P(row),
            P("x"),
        ),
        out_specs=(P(row, "x"), P(row, "x"), P(row), P("x"), P(row), P("x")),
        check_vma=False,
    )
```

```python
import jax
import jax.numpy as jnp
from jax import lax
from jax.experimental import pallas as pl
from jax.experimental.pallas import tpu as pltpu
from jax.sharding import Mesh, PartitionSpec as P

D = 4096
FF = 16384

EPSILON = 1e-30
DECAY = 1.0 - 100.0 ** (-0.8)

ROWS_IN, COLS_IN = 64, 4096
ROWS_OUT, COLS_OUT = 256, 1024
HALF_IN, HALF_OUT = COLS_IN // 2, COLS_OUT // 2
PACK = (128, 2048)
BLOCKS = ROWS_OUT // 64
TILES_IN = HALF_IN // 128
TILES_OUT = HALF_OUT // 128

F32 = jnp.float32
VMEM = pl.BlockSpec(memory_space=pltpu.VMEM)
HBM = pl.BlockSpec(memory_space=pltpu.HBM)
PARAMS = pltpu.CompilerParams(vmem_limit_bytes=16 * 1024 * 1024)


def lanes(tile):
    return pl.ds(tile * 128, 128)


def half_copies(grad_in, grad_out, half, block_in, block_out, sems):
    columns_in = pl.ds(pl.multiple_of(half * HALF_IN, 128), HALF_IN)
    columns_out = pl.ds(pl.multiple_of(half * HALF_OUT, 128), HALF_OUT)
    return (
        pltpu.make_async_copy(grad_in.at[:, columns_in], block_in, sems.at[0]),
        pltpu.make_async_copy(grad_out.at[:, columns_out], block_out, sems.at[1]),
    )


HALF_SCRATCH = [
    pltpu.VMEM((ROWS_IN, HALF_IN), jnp.bfloat16),
    pltpu.VMEM((ROWS_OUT, HALF_OUT), jnp.bfloat16),
]


def fetch_kernel(grad_in, grad_out, *refs):
    first, other_in, other_out, sems = refs[4], refs[9], refs[10], refs[11]
    copies = half_copies(grad_in, grad_out, 1 - lax.axis_index("dp"), other_in, other_out, sems)
    small = [pltpu.make_async_copy(refs[at], refs[5 + at], sems.at[2 + at]) for at in range(4)]
    for copy in (*copies, *small):
        copy.start()
    copies[0].wait()
    first[0:64, :] = other_in[...].astype(F32)
    copies[1].wait()
    for k in range(BLOCKS):
        first[64:128, pl.ds(k * HALF_OUT, HALF_OUT)] = other_out[pl.ds(64 * k, 64), :].astype(F32)
    for copy in small:
        copy.wait()


def fetch(grad_in, grad_out, *factors):
    return pl.pallas_call(
        fetch_kernel,
        out_shape=tuple(jax.ShapeDtypeStruct(shape, F32) for shape in (PACK, *(x.shape for x in factors))),
        in_specs=[HBM] * 6,
        out_specs=(VMEM,) * 5,
        scratch_shapes=HALF_SCRATCH + [pltpu.SemaphoreType.DMA((6,))],
        compiler_params=PARAMS,
        name="fetch",
    )(grad_in, grad_out, *factors)


def widen_kernel(grad_in, grad_out, packed):
    half = lax.axis_index("dp")
    packed[0:64, :] = grad_in[:, pl.ds(pl.multiple_of(half * HALF_IN, 128), HALF_IN)].astype(F32)
    columns = pl.ds(pl.multiple_of(half * HALF_OUT, 128), HALF_OUT)
    for k in range(BLOCKS):
        packed[64:128, pl.ds(k * HALF_OUT, HALF_OUT)] = grad_out[pl.ds(64 * k, 64), columns].astype(F32)


def widen_own(grad_in, grad_out):
    return pl.pallas_call(
        widen_kernel,
        out_shape=jax.ShapeDtypeStruct(PACK, F32),
        in_specs=[VMEM] * 2,
        out_specs=VMEM,
        compiler_params=PARAMS,
        name="widen_own",
    )(grad_in, grad_out)


def rows_kernel(own, received, summed, row_sums):
    def lane_partial(row, tiles):
        total = None
        for tile in tiles:
            value = own[pl.ds(row, 64), lanes(tile)] + received[pl.ds(row, 64), lanes(tile)]
            summed[pl.ds(row, 64), lanes(tile)] = value
            square = value * value
            total = square if total is None else total + square
        return total

    def to_lanes(upper, lower):
        return jnp.sum(jnp.concatenate([upper, lower], axis=0).T, axis=0, keepdims=True)

    part = lane_partial(0, range(TILES_IN))
    vectors = [to_lanes(part, jnp.zeros_like(part))]
    for pair in range(BLOCKS // 2):
        upper, lower = (
            lane_partial(64, range(k * TILES_OUT, (k + 1) * TILES_OUT)) for k in (2 * pair, 2 * pair + 1)
        )
        vectors.append(to_lanes(upper, lower))
    for at, vector in enumerate(vectors):
        for peer in range(8):
            row_sums[peer, :, lanes(at)] = vector


def row_sums_of(own, received):
    return pl.pallas_call(
        rows_kernel,
        out_shape=(jax.ShapeDtypeStruct(PACK, F32), jax.ShapeDtypeStruct((8, 1, 384), F32)),
        in_specs=[VMEM, VMEM],
        out_specs=(VMEM, VMEM),
        compiler_params=PARAMS,
        name="row_sums",
    )(own, received)


def columns_kernel(row_sums, rows_in, rows_out, summed, scaled, row_scale, new_in, new_out, sends):
    total = jnp.sum(row_sums[...], axis=0)
    fresh_in = DECAY * rows_in[...] + (1.0 - DECAY) * (total[:, 0:64] * (1.0 / FF) + EPSILON)
    fresh_out = DECAY * rows_out[...] + (1.0 - DECAY) * (total[:, 128:384] * (1.0 / D) + EPSILON)
    new_in[...] = fresh_in
    new_out[...] = fresh_out
    root_in = lax.rsqrt(fresh_in)
    root_out = lax.rsqrt(fresh_out)

    def to_rows(vector):
        return jnp.broadcast_to(vector, (128, 128)).T

    row_scale[0:64, :] = to_rows(jnp.concatenate([root_in, root_in], axis=1))[0:64, :]
    row_scale[64:192, :] = to_rows(root_out[:, 0:128])
    row_scale[192:320, :] = to_rows(root_out[:, 128:256])

    def column(row, scale_row, tile):
        value = summed[pl.ds(row, 64), lanes(tile)]
        weighted = value * row_scale[pl.ds(scale_row, 64), :]
        scaled[pl.ds(row, 64), lanes(tile)] = weighted
        return (
            jnp.sum((value * value).reshape(8, 8, 128), axis=0),
            jnp.sum((weighted * weighted).reshape(8, 8, 128), axis=0),
        )

    def fold(value):
        return jnp.sum(value, axis=0, keepdims=True)

    def send(chunk, row, vector):
        for peer in range(chunk, 8, 2):
            sends[peer, row // 4, row % 4 : row % 4 + 1, :] = vector

    for tile in range(TILES_IN):
        plain, weighted = column(0, 0, tile)
        send(tile // 8, tile % 8, fold(plain))
        send(tile // 8, 8 + tile % 8, fold(weighted))
    for tile in range(TILES_OUT):
        plain, weighted = column(64, 64, tile)
        for k in range(1, BLOCKS):
            more = column(64, 64 + 64 * k, k * TILES_OUT + tile)
            plain, weighted = plain + more[0], weighted + more[1]
        send(tile // 2, 16 + tile % 2, fold(plain))
        send(tile // 2, 18 + tile % 2, fold(weighted))


def column_sums_of(row_sums, rows_in, rows_out, summed):
    return pl.pallas_call(
        columns_kernel,
        out_shape=(
            jax.ShapeDtypeStruct(PACK, F32),
            jax.ShapeDtypeStruct((320, 128), F32),
            jax.ShapeDtypeStruct((1, ROWS_IN), F32),
            jax.ShapeDtypeStruct((1, ROWS_OUT), F32),
            jax.ShapeDtypeStruct((8, 5, 4, 128), F32),
        ),
        in_specs=[VMEM] * 4,
        out_specs=(VMEM,) * 5,
        compiler_params=PARAMS,
        name="column_sums",
    )(row_sums, rows_in, rows_out, summed)


def total_kernel(sums, sends):
    total = sums[0]
    for peer in range(1, 8):
        total = total + sums[peer]
    for peer in range(8):
        sends[peer] = total


def total_of(sums):
    return pl.pallas_call(
        total_kernel,
        out_shape=jax.ShapeDtypeStruct((8, 5, 4, 128), F32),
        in_specs=[VMEM],
        out_specs=VMEM,
        compiler_params=PARAMS,
        name="total",
    )(sums)


def factors_kernel(sums, cols_in, cols_out, sends):
    chunk = lax.axis_index("dp") * 2 + lax.axis_index("pair")
    total = sums[0]
    for peer in range(1, 8):
        total = total + sums[peer]
    energy_in = jnp.zeros((1, 128), F32)
    for part in range(2):
        new_in = DECAY * cols_in[chunk * 2 + part] + (1.0 - DECAY) * (total[part] * (1.0 / D) + EPSILON)
        energy_in += jnp.sum(total[2 + part] / new_in, axis=0, keepdims=True)
        for peer in range(16):
            sends[peer, part] = new_in
    new_out = DECAY * cols_out[chunk] + (1.0 - DECAY) * (total[4, 0:2] * (1.0 / FF) + EPSILON)
    energy_out = jnp.sum(total[4, 2:4] / new_out, axis=0, keepdims=True)
    last = jnp.concatenate([new_out, energy_in, energy_out], axis=0)
    for peer in range(16):
        sends[peer, 2] = last


def factors_of(sums, cols_in, cols_out):
    return pl.pallas_call(
        factors_kernel,
        out_shape=jax.ShapeDtypeStruct((16, 3, 4, 128), F32),
        in_specs=[VMEM] * 3,
        out_specs=VMEM,
        compiler_params=PARAMS,
        name="column_factors",
    )(sums, cols_in, cols_out)


def scales_kernel(factors, cols, scales):
    my_x = lax.axis_index("x")
    energies = factors[0, 2]
    for peer in range(1, 16):
        energies = energies + factors[peer, 2]

    def limit(row):
        energy = jnp.sum(energies[row : row + 1, :], axis=1, keepdims=True)
        return 1.0 / jnp.maximum(1.0, jnp.sqrt(energy * (1.0 / (D * FF))))

    limit_in, limit_out = limit(2), limit(3)
    for chunk in range(4):
        owner = chunk * 4 + my_x
        for part in range(2):
            here = factors[owner, part]
            cols[pl.ds(chunk * 8 + part * 4, 4), :] = here
            scales[pl.ds(chunk * 8 + part * 4, 4), :] = lax.rsqrt(here) * limit_in
        here = factors[owner, 2, 0:2, :]
        cols[pl.ds(32 + chunk * 2, 2), :] = here
        scales[pl.ds(32 + chunk * 2, 2), :] = lax.rsqrt(here) * limit_out


def scales_of(factors):
    return pl.pallas_call(
        scales_kernel,
        out_shape=(jax.ShapeDtypeStruct((40, 128), F32), jax.ShapeDtypeStruct((40, 128), F32)),
        in_specs=[VMEM],
        out_specs=(VMEM, VMEM),
        compiler_params=PARAMS,
        name="scales",
    )(factors)


def update_kernel(
    cols, scales, scaled, row_scale, first, received, rows_in_new, rows_out_new,
    update_in, update_out, rows_in, rows_out, cols_in, cols_out,
    buf_in, buf_out, sems,
):
    own_half = lax.axis_index("dp")
    copies = []

    def write(source, target):
        copy = pltpu.make_async_copy(source, target, sems.at[len(copies)])
        copy.start()
        copies.append(copy)

    def block(buffer, target, offset, width, start):
        write(
            buffer.at[:, pl.ds(start, width)],
            target.at[:, pl.ds(pl.multiple_of(offset + start, 128), width)],
        )

    write(cols.at[0:32, :], cols_in)
    write(cols.at[32:40, :], cols_out)
    write(rows_in_new, rows_in)
    write(rows_out_new, rows_out)
    for which, half in ((0, own_half), (1, 1 - own_half)):

        def value(row, scale_row, tile):
            if which == 0:
                return scaled[pl.ds(row, 64), lanes(tile)]
            both = first[pl.ds(row, 64), lanes(tile)] + received[pl.ds(row, 64), lanes(tile)]
            return both * row_scale[pl.ds(scale_row, 64), :]

        for tile in range(TILES_IN):
            buf_in[which, :, lanes(tile)] = value(0, 0, tile) * scales[pl.ds(half * TILES_IN + tile, 1), :]
            if tile % 8 == 7:
                block(buf_in.at[which], update_in, half * HALF_IN, 1024, (tile - 7) * 128)
        for tile in range(TILES_OUT):
            scale = scales[pl.ds(32 + half * TILES_OUT + tile, 1), :]
            for k in range(BLOCKS):
                buf_out[which, pl.ds(64 * k, 64), lanes(tile)] = (
                    value(64, 64 + 64 * k, k * TILES_OUT + tile) * scale
                )
            if tile % 2 == 1:
                block(buf_out.at[which], update_out, half * HALF_OUT, 256, (tile - 1) * 128)
    for copy in copies:
        copy.wait()


def update_of(*operands):
    return pl.pallas_call(
        update_kernel,
        out_shape=(
            jax.ShapeDtypeStruct((ROWS_IN, COLS_IN), F32),
            jax.ShapeDtypeStruct((ROWS_OUT, COLS_OUT), F32),
            jax.ShapeDtypeStruct((1, ROWS_IN), F32),
            jax.ShapeDtypeStruct((1, ROWS_OUT), F32),
            jax.ShapeDtypeStruct((COLS_IN // 128, 128), F32),
            jax.ShapeDtypeStruct((COLS_OUT // 128, 128), F32),
        ),
        in_specs=[VMEM] * 8,
        out_specs=(HBM,) * 6,
        scratch_shapes=[
            pltpu.VMEM((2, ROWS_IN, HALF_IN), F32),
            pltpu.VMEM((2, ROWS_OUT, HALF_OUT), F32),
            pltpu.SemaphoreType.DMA((12,)),
        ],
        compiler_params=PARAMS,
        name="update",
    )(*operands)


def keep_in_hbm(x):
    return pltpu.with_memory_space_constraint(x, pltpu.HBM)


def per_device(grad_in, grad_out, rows_in, cols_in, rows_out, cols_out):
    swap = [(0, 1), (1, 0)]
    grad_in, grad_out = grad_in[0], grad_out[0]
    first, rows_in, rows_out, cols_in, cols_out = fetch(
        *map(
            keep_in_hbm,
            (
                grad_in,
                grad_out,
                rows_in.reshape(1, ROWS_IN),
                rows_out.reshape(1, ROWS_OUT),
                cols_in.reshape(8, 4, 128),
                cols_out.reshape(4, 2, 128),
            ),
        )
    )
    arrived_own = lax.ppermute(first, "dp", swap)
    own = widen_own(grad_in, grad_out)
    arrived_other = lax.ppermute(own, "dp", swap)

    summed, row_sums = row_sums_of(own, arrived_own)
    row_sums = lax.all_to_all(row_sums, ("dp", "x"), 0, 0)
    scaled, row_scale, new_rows_in, new_rows_out, sums = column_sums_of(row_sums, rows_in, rows_out, summed)
    sums = lax.all_to_all(sums, ("y", "pair"), 0, 0)
    sums = lax.all_to_all(total_of(sums), "z", 0, 0)
    factors = lax.all_to_all(factors_of(sums, cols_in, cols_out), ("dp", "pair", "x"), 0, 0)
    cols, scales = scales_of(factors)
    update_in, update_out, new_rows_in, new_rows_out, new_cols_in, new_cols_out = update_of(
        cols, scales, scaled, row_scale, first, arrived_other, new_rows_in, new_rows_out
    )
    return (
        update_in,
        update_out,
        new_rows_in.reshape(ROWS_IN),
        new_cols_in.reshape(COLS_IN),
        new_rows_out.reshape(ROWS_OUT),
        new_cols_out.reshape(COLS_OUT),
    )


def solution(mesh):
    fine = Mesh(mesh.devices.reshape(2, 8, 4, 2, 4), ("dp", "z", "y", "pair", "x"))
    row = ("z", "y", "pair")
    return jax.shard_map(
        per_device,
        mesh=fine,
        in_specs=(
            P("dp", row, "x"),
            P("dp", row, "x"),
            P(row),
            P("x"),
            P(row),
            P("x"),
        ),
        out_specs=(P(row, "x"), P(row, "x"), P(row), P("x"), P(row), P("x")),
        check_vma=False,
    )
```

```python
import jax
import jax.numpy as jnp
from jax import lax
from jax.experimental import pallas as pl
from jax.experimental.pallas import tpu as pltpu
from jax.sharding import Mesh, PartitionSpec as P

D = 4096
FF = 16384

EPSILON = 1e-30
DECAY = 1.0 - 100.0 ** (-0.8)

ROWS_IN, COLS_IN = 64, 4096
ROWS_OUT, COLS_OUT = 256, 1024
HALF_IN, HALF_OUT = COLS_IN // 2, COLS_OUT // 2
PACK = (128, 2048)
BLOCKS = ROWS_OUT // 64
TILES_IN = HALF_IN // 128
TILES_OUT = HALF_OUT // 128

F32 = jnp.float32
VMEM = pl.BlockSpec(memory_space=pltpu.VMEM)
HBM = pl.BlockSpec(memory_space=pltpu.HBM)
PARAMS = pltpu.CompilerParams(vmem_limit_bytes=16 * 1024 * 1024)


def lanes(tile):
    return pl.ds(tile * 128, 128)


def half_copies(grad_in, grad_out, half, block_in, block_out, sems):
    columns_in = pl.ds(pl.multiple_of(half * HALF_IN, 128), HALF_IN)
    columns_out = pl.ds(pl.multiple_of(half * HALF_OUT, 128), HALF_OUT)
    return (
        pltpu.make_async_copy(grad_in.at[:, columns_in], block_in, sems.at[0]),
        pltpu.make_async_copy(grad_out.at[:, columns_out], block_out, sems.at[1]),
    )


HALF_SCRATCH = [
    pltpu.VMEM((ROWS_IN, HALF_IN), jnp.bfloat16),
    pltpu.VMEM((ROWS_OUT, HALF_OUT), jnp.bfloat16),
]


def fetch_kernel(grad_in, grad_out, *refs):
    first, other_in, other_out, sems = refs[4], refs[9], refs[10], refs[11]
    copies = half_copies(grad_in, grad_out, 1 - lax.axis_index("dp"), other_in, other_out, sems)
    small = [pltpu.make_async_copy(refs[at], refs[5 + at], sems.at[2 + at]) for at in range(4)]
    for copy in (*copies, *small):
        copy.start()
    copies[0].wait()
    first[0:64, :] = other_in[...].astype(F32)
    copies[1].wait()
    for k in range(BLOCKS):
        first[64:128, pl.ds(k * HALF_OUT, HALF_OUT)] = other_out[pl.ds(64 * k, 64), :].astype(F32)
    for copy in small:
        copy.wait()


def fetch(grad_in, grad_out, *factors):
    return pl.pallas_call(
        fetch_kernel,
        out_shape=tuple(jax.ShapeDtypeStruct(shape, F32) for shape in (PACK, *(x.shape for x in factors))),
        in_specs=[HBM] * 6,
        out_specs=(VMEM,) * 5,
        scratch_shapes=HALF_SCRATCH + [pltpu.SemaphoreType.DMA((6,))],
        compiler_params=PARAMS,
        name="fetch",
    )(grad_in, grad_out, *factors)


def widen_kernel(grad_in, grad_out, packed):
    half = lax.axis_index("dp")
    packed[0:64, :] = grad_in[:, pl.ds(pl.multiple_of(half * HALF_IN, 128), HALF_IN)].astype(F32)
    columns = pl.ds(pl.multiple_of(half * HALF_OUT, 128), HALF_OUT)
    for k in range(BLOCKS):
        packed[64:128, pl.ds(k * HALF_OUT, HALF_OUT)] = grad_out[pl.ds(64 * k, 64), columns].astype(F32)


def widen_own(grad_in, grad_out):
    return pl.pallas_call(
        widen_kernel,
        out_shape=jax.ShapeDtypeStruct(PACK, F32),
        in_specs=[VMEM] * 2,
        out_specs=VMEM,
        compiler_params=PARAMS,
        name="widen_own",
    )(grad_in, grad_out)


def rows_kernel(own, received, summed, row_sums):
    def lane_partial(row, tiles):
        total = None
        for tile in tiles:
            value = own[pl.ds(row, 64), lanes(tile)] + received[pl.ds(row, 64), lanes(tile)]
            summed[pl.ds(row, 64), lanes(tile)] = value
            square = value * value
            total = square if total is None else total + square
        return total

    def to_lanes(upper, lower):
        return jnp.sum(jnp.concatenate([upper, lower], axis=0).T, axis=0, keepdims=True)

    part = lane_partial(0, range(TILES_IN))
    vectors = [to_lanes(part, jnp.zeros_like(part))]
    for pair in range(BLOCKS // 2):
        upper, lower = (
            lane_partial(64, range(k * TILES_OUT, (k + 1) * TILES_OUT)) for k in (2 * pair, 2 * pair + 1)
        )
        vectors.append(to_lanes(upper, lower))
    for at, vector in enumerate(vectors):
        for peer in range(8):
            row_sums[peer, :, lanes(at)] = vector


def row_sums_of(own, received):
    return pl.pallas_call(
        rows_kernel,
        out_shape=(jax.ShapeDtypeStruct(PACK, F32), jax.ShapeDtypeStruct((8, 1, 384), F32)),
        in_specs=[VMEM, VMEM],
        out_specs=(VMEM, VMEM),
        compiler_params=PARAMS,
        name="row_sums",
    )(own, received)


def columns_kernel(row_sums, rows_in, rows_out, summed, scaled, row_scale, new_in, new_out, sends):
    total = jnp.sum(row_sums[...], axis=0)
    fresh_in = DECAY * rows_in[...] + (1.0 - DECAY) * (total[:, 0:64] * (1.0 / FF) + EPSILON)
    fresh_out = DECAY * rows_out[...] + (1.0 - DECAY) * (total[:, 128:384] * (1.0 / D) + EPSILON)
    new_in[...] = fresh_in
    new_out[...] = fresh_out
    root_in = lax.rsqrt(fresh_in)
    root_out = lax.rsqrt(fresh_out)

    def to_rows(vector):
        return jnp.broadcast_to(vector, (128, 128)).T

    row_scale[0:64, :] = to_rows(jnp.concatenate([root_in, root_in], axis=1))[0:64, :]
    row_scale[64:192, :] = to_rows(root_out[:, 0:128])
    row_scale[192:320, :] = to_rows(root_out[:, 128:256])

    def column(row, scale_row, tile):
        value = summed[pl.ds(row, 64), lanes(tile)]
        weighted = value * row_scale[pl.ds(scale_row, 64), :]
        scaled[pl.ds(row, 64), lanes(tile)] = weighted
        return (
            jnp.sum((value * value).reshape(8, 8, 128), axis=0),
            jnp.sum((weighted * weighted).reshape(8, 8, 128), axis=0),
        )

    def fold(value):
        return jnp.sum(value, axis=0, keepdims=True)

    def send(chunk, row, vector):
        for peer in range(4 * chunk, 4 * chunk + 4):
            sends[peer, row // 4, row % 4 : row % 4 + 1, :] = vector

    for tile in range(TILES_IN):
        plain, weighted = column(0, 0, tile)
        send(tile // 8, tile % 8, fold(plain))
        send(tile // 8, 8 + tile % 8, fold(weighted))
    for tile in range(TILES_OUT):
        plain, weighted = column(64, 64, tile)
        for k in range(1, BLOCKS):
            more = column(64, 64 + 64 * k, k * TILES_OUT + tile)
            plain, weighted = plain + more[0], weighted + more[1]
        send(tile // 2, 16 + tile % 2, fold(plain))
        send(tile // 2, 18 + tile % 2, fold(weighted))


def column_sums_of(row_sums, rows_in, rows_out, summed):
    return pl.pallas_call(
        columns_kernel,
        out_shape=(
            jax.ShapeDtypeStruct(PACK, F32),
            jax.ShapeDtypeStruct((320, 128), F32),
            jax.ShapeDtypeStruct((1, ROWS_IN), F32),
            jax.ShapeDtypeStruct((1, ROWS_OUT), F32),
            jax.ShapeDtypeStruct((8, 5, 4, 128), F32),
        ),
        in_specs=[VMEM] * 4,
        out_specs=(VMEM,) * 5,
        compiler_params=PARAMS,
        name="column_sums",
    )(row_sums, rows_in, rows_out, summed)


def total_kernel(sums, sends):
    total = sums[0]
    for peer in range(1, 8):
        total = total + sums[peer]
    for peer in range(8):
        sends[peer] = total


def total_of(sums):
    return pl.pallas_call(
        total_kernel,
        out_shape=jax.ShapeDtypeStruct((8, 5, 4, 128), F32),
        in_specs=[VMEM],
        out_specs=VMEM,
        compiler_params=PARAMS,
        name="total",
    )(sums)


def factors_kernel(sums, cols_in, cols_out, sends):
    chunk = lax.axis_index("dp") * 2 + lax.axis_index("pair")
    total = sums[0]
    for peer in range(1, 8):
        total = total + sums[peer]
    energy_in = jnp.zeros((1, 128), F32)
    for part in range(2):
        new_in = DECAY * cols_in[chunk * 2 + part] + (1.0 - DECAY) * (total[part] * (1.0 / D) + EPSILON)
        energy_in += jnp.sum(total[2 + part] / new_in, axis=0, keepdims=True)
        for peer in range(16):
            sends[peer, part] = new_in
    new_out = DECAY * cols_out[chunk] + (1.0 - DECAY) * (total[4, 0:2] * (1.0 / FF) + EPSILON)
    energy_out = jnp.sum(total[4, 2:4] / new_out, axis=0, keepdims=True)
    last = jnp.concatenate([new_out, energy_in, energy_out], axis=0)
    for peer in range(16):
        sends[peer, 2] = last


def factors_of(sums, cols_in, cols_out):
    return pl.pallas_call(
        factors_kernel,
        out_shape=jax.ShapeDtypeStruct((16, 3, 4, 128), F32),
        in_specs=[VMEM] * 3,
        out_specs=VMEM,
        compiler_params=PARAMS,
        name="column_factors",
    )(sums, cols_in, cols_out)


def scales_kernel(factors, cols, scales):
    my_x = lax.axis_index("x")
    energies = factors[0, 2]
    for peer in range(1, 16):
        energies = energies + factors[peer, 2]

    def limit(row):
        energy = jnp.sum(energies[row : row + 1, :], axis=1, keepdims=True)
        return 1.0 / jnp.maximum(1.0, jnp.sqrt(energy * (1.0 / (D * FF))))

    limit_in, limit_out = limit(2), limit(3)
    for chunk in range(4):
        owner = my_x * 4 + chunk % 2 * 2 + chunk // 2
        for part in range(2):
            here = factors[owner, part]
            cols[pl.ds(chunk * 8 + part * 4, 4), :] = here
            scales[pl.ds(chunk * 8 + part * 4, 4), :] = lax.rsqrt(here) * limit_in
        here = factors[owner, 2, 0:2, :]
        cols[pl.ds(32 + chunk * 2, 2), :] = here
        scales[pl.ds(32 + chunk * 2, 2), :] = lax.rsqrt(here) * limit_out


def scales_of(factors):
    return pl.pallas_call(
        scales_kernel,
        out_shape=(jax.ShapeDtypeStruct((40, 128), F32), jax.ShapeDtypeStruct((40, 128), F32)),
        in_specs=[VMEM],
        out_specs=(VMEM, VMEM),
        compiler_params=PARAMS,
        name="scales",
    )(factors)


def update_kernel(
    cols, scales, scaled, row_scale, first, received, rows_in_new, rows_out_new,
    update_in, update_out, rows_in, rows_out, cols_in, cols_out,
    buf_in, buf_out, sems,
):
    own_half = lax.axis_index("dp")
    copies = []

    def write(source, target):
        copy = pltpu.make_async_copy(source, target, sems.at[len(copies)])
        copy.start()
        copies.append(copy)

    def block(buffer, target, offset, width, start):
        write(
            buffer.at[:, pl.ds(start, width)],
            target.at[:, pl.ds(pl.multiple_of(offset + start, 128), width)],
        )

    write(cols.at[0:32, :], cols_in)
    write(cols.at[32:40, :], cols_out)
    write(rows_in_new, rows_in)
    write(rows_out_new, rows_out)
    for which, half in ((0, own_half), (1, 1 - own_half)):

        def value(row, scale_row, tile):
            if which == 0:
                return scaled[pl.ds(row, 64), lanes(tile)]
            both = first[pl.ds(row, 64), lanes(tile)] + received[pl.ds(row, 64), lanes(tile)]
            return both * row_scale[pl.ds(scale_row, 64), :]

        for tile in range(TILES_IN):
            buf_in[which, :, lanes(tile)] = value(0, 0, tile) * scales[pl.ds(half * TILES_IN + tile, 1), :]
            if tile % 8 == 7:
                block(buf_in.at[which], update_in, half * HALF_IN, 1024, (tile - 7) * 128)
        for tile in range(TILES_OUT):
            scale = scales[pl.ds(32 + half * TILES_OUT + tile, 1), :]
            for k in range(BLOCKS):
                buf_out[which, pl.ds(64 * k, 64), lanes(tile)] = (
                    value(64, 64 + 64 * k, k * TILES_OUT + tile) * scale
                )
            if tile % 2 == 1:
                block(buf_out.at[which], update_out, half * HALF_OUT, 256, (tile - 1) * 128)
    for copy in copies:
        copy.wait()


def update_of(*operands):
    return pl.pallas_call(
        update_kernel,
        out_shape=(
            jax.ShapeDtypeStruct((ROWS_IN, COLS_IN), F32),
            jax.ShapeDtypeStruct((ROWS_OUT, COLS_OUT), F32),
            jax.ShapeDtypeStruct((1, ROWS_IN), F32),
            jax.ShapeDtypeStruct((1, ROWS_OUT), F32),
            jax.ShapeDtypeStruct((COLS_IN // 128, 128), F32),
            jax.ShapeDtypeStruct((COLS_OUT // 128, 128), F32),
        ),
        in_specs=[VMEM] * 8,
        out_specs=(HBM,) * 6,
        scratch_shapes=[
            pltpu.VMEM((2, ROWS_IN, HALF_IN), F32),
            pltpu.VMEM((2, ROWS_OUT, HALF_OUT), F32),
            pltpu.SemaphoreType.DMA((12,)),
        ],
        compiler_params=PARAMS,
        name="update",
    )(*operands)


def keep_in_hbm(x):
    return pltpu.with_memory_space_constraint(x, pltpu.HBM)


def per_device(grad_in, grad_out, rows_in, cols_in, rows_out, cols_out):
    swap = [(0, 1), (1, 0)]
    grad_in, grad_out = grad_in[0], grad_out[0]
    first, rows_in, rows_out, cols_in, cols_out = fetch(
        *map(
            keep_in_hbm,
            (
                grad_in,
                grad_out,
                rows_in.reshape(1, ROWS_IN),
                rows_out.reshape(1, ROWS_OUT),
                cols_in.reshape(8, 4, 128),
                cols_out.reshape(4, 2, 128),
            ),
        )
    )
    arrived_own = lax.ppermute(first, "dp", swap)
    own = widen_own(grad_in, grad_out)
    arrived_other = lax.ppermute(own, "dp", swap)

    summed, row_sums = row_sums_of(own, arrived_own)
    row_sums = lax.all_to_all(row_sums, ("x", "dp"), 0, 0)
    scaled, row_scale, new_rows_in, new_rows_out, sums = column_sums_of(row_sums, rows_in, rows_out, summed)
    sums = lax.all_to_all(sums, ("pair", "y"), 0, 0)
    sums = lax.all_to_all(total_of(sums), "z", 0, 0)
    factors = lax.all_to_all(factors_of(sums, cols_in, cols_out), ("x", "pair", "dp"), 0, 0)
    cols, scales = scales_of(factors)
    update_in, update_out, new_rows_in, new_rows_out, new_cols_in, new_cols_out = update_of(
        cols, scales, scaled, row_scale, first, arrived_other, new_rows_in, new_rows_out
    )
    return (
        update_in,
        update_out,
        new_rows_in.reshape(ROWS_IN),
        new_cols_in.reshape(COLS_IN),
        new_rows_out.reshape(ROWS_OUT),
        new_cols_out.reshape(COLS_OUT),
    )


def solution(mesh):
    fine = Mesh(mesh.devices.reshape(2, 8, 4, 2, 4), ("dp", "z", "y", "pair", "x"))
    row = ("z", "y", "pair")
    return jax.shard_map(
        per_device,
        mesh=fine,
        in_specs=(
            P("dp", row, "x"),
            P("dp", row, "x"),
            P(row),
            P("x"),
            P(row),
            P("x"),
        ),
        out_specs=(P(row, "x"), P(row, "x"), P(row), P("x"), P(row), P("x")),
        check_vma=False,
    )
```

```python
import jax
import jax.numpy as jnp
from jax import lax
from jax.experimental import pallas as pl
from jax.experimental.pallas import tpu as pltpu
from jax.sharding import Mesh, PartitionSpec as P

D = 4096
FF = 16384

EPSILON = 1e-30
DECAY = 1.0 - 100.0 ** (-0.8)

ROWS_IN, COLS_IN = 64, 4096
ROWS_OUT, COLS_OUT = 256, 1024
HALF_IN, HALF_OUT = COLS_IN // 2, COLS_OUT // 2
PACK = (128, 2048)
BLOCKS = ROWS_OUT // 64
TILES_IN = HALF_IN // 128
TILES_OUT = HALF_OUT // 128

F32 = jnp.float32
VMEM = pl.BlockSpec(memory_space=pltpu.VMEM)
HBM = pl.BlockSpec(memory_space=pltpu.HBM)
PARAMS = pltpu.CompilerParams(vmem_limit_bytes=16 * 1024 * 1024)


def lanes(tile):
    return pl.ds(tile * 128, 128)


def half_copies(grad_in, grad_out, half, block_in, block_out, sems):
    columns_in = pl.ds(pl.multiple_of(half * HALF_IN, 128), HALF_IN)
    columns_out = pl.ds(pl.multiple_of(half * HALF_OUT, 128), HALF_OUT)
    return (
        pltpu.make_async_copy(grad_in.at[:, columns_in], block_in, sems.at[0]),
        pltpu.make_async_copy(grad_out.at[:, columns_out], block_out, sems.at[1]),
    )


HALF_SCRATCH = [
    pltpu.VMEM((ROWS_IN, HALF_IN), jnp.bfloat16),
    pltpu.VMEM((ROWS_OUT, HALF_OUT), jnp.bfloat16),
]


def fetch_kernel(grad_in, grad_out, *refs):
    first, other_in, other_out, sems = refs[4], refs[9], refs[10], refs[11]
    copies = half_copies(grad_in, grad_out, 1 - lax.axis_index("dp"), other_in, other_out, sems)
    small = [pltpu.make_async_copy(refs[at], refs[5 + at], sems.at[2 + at]) for at in range(4)]
    for copy in (*copies, *small):
        copy.start()
    copies[0].wait()
    first[0:64, :] = other_in[...].astype(F32)
    copies[1].wait()
    for k in range(BLOCKS):
        first[64:128, pl.ds(k * HALF_OUT, HALF_OUT)] = other_out[pl.ds(64 * k, 64), :].astype(F32)
    for copy in small:
        copy.wait()


def fetch(grad_in, grad_out, *factors):
    return pl.pallas_call(
        fetch_kernel,
        out_shape=tuple(jax.ShapeDtypeStruct(shape, F32) for shape in (PACK, *(x.shape for x in factors))),
        in_specs=[HBM] * 6,
        out_specs=(VMEM,) * 5,
        scratch_shapes=HALF_SCRATCH + [pltpu.SemaphoreType.DMA((6,))],
        compiler_params=PARAMS,
        name="fetch",
    )(grad_in, grad_out, *factors)


def widen_kernel(grad_in, grad_out, packed):
    half = lax.axis_index("dp")
    packed[0:64, :] = grad_in[:, pl.ds(pl.multiple_of(half * HALF_IN, 128), HALF_IN)].astype(F32)
    columns = pl.ds(pl.multiple_of(half * HALF_OUT, 128), HALF_OUT)
    for k in range(BLOCKS):
        packed[64:128, pl.ds(k * HALF_OUT, HALF_OUT)] = grad_out[pl.ds(64 * k, 64), columns].astype(F32)


def widen_own(grad_in, grad_out):
    return pl.pallas_call(
        widen_kernel,
        out_shape=jax.ShapeDtypeStruct(PACK, F32),
        in_specs=[VMEM] * 2,
        out_specs=VMEM,
        compiler_params=PARAMS,
        name="widen_own",
    )(grad_in, grad_out)


def rows_kernel(own, received, summed, row_sums):
    def lane_partial(row, tiles):
        total = None
        for tile in tiles:
            value = own[pl.ds(row, 64), lanes(tile)] + received[pl.ds(row, 64), lanes(tile)]
            summed[pl.ds(row, 64), lanes(tile)] = value
            square = value * value
            total = square if total is None else total + square
        return total

    def to_lanes(upper, lower):
        return jnp.sum(jnp.concatenate([upper, lower], axis=0).T, axis=0, keepdims=True)

    part = lane_partial(0, range(TILES_IN))
    vectors = [to_lanes(part, jnp.zeros_like(part))]
    for pair in range(BLOCKS // 2):
        upper, lower = (
            lane_partial(64, range(k * TILES_OUT, (k + 1) * TILES_OUT)) for k in (2 * pair, 2 * pair + 1)
        )
        vectors.append(to_lanes(upper, lower))
    for at, vector in enumerate(vectors):
        for peer in range(8):
            row_sums[peer, :, lanes(at)] = vector


def row_sums_of(own, received):
    return pl.pallas_call(
        rows_kernel,
        out_shape=(jax.ShapeDtypeStruct(PACK, F32), jax.ShapeDtypeStruct((8, 1, 384), F32)),
        in_specs=[VMEM, VMEM],
        out_specs=(VMEM, VMEM),
        compiler_params=PARAMS,
        name="row_sums",
    )(own, received)


def columns_kernel(row_sums, rows_in, rows_out, summed, scaled, row_scale, new_in, new_out, sends):
    total = jnp.sum(row_sums[...], axis=0)
    fresh_in = DECAY * rows_in[...] + (1.0 - DECAY) * (total[:, 0:64] * (1.0 / FF) + EPSILON)
    fresh_out = DECAY * rows_out[...] + (1.0 - DECAY) * (total[:, 128:384] * (1.0 / D) + EPSILON)
    new_in[...] = fresh_in
    new_out[...] = fresh_out
    root_in = lax.rsqrt(fresh_in)
    root_out = lax.rsqrt(fresh_out)

    def to_rows(vector):
        return jnp.broadcast_to(vector, (128, 128)).T

    row_scale[0:64, :] = to_rows(jnp.concatenate([root_in, root_in], axis=1))[0:64, :]
    row_scale[64:192, :] = to_rows(root_out[:, 0:128])
    row_scale[192:320, :] = to_rows(root_out[:, 128:256])

    def column(row, scale_row, tile):
        value = summed[pl.ds(row, 64), lanes(tile)]
        weighted = value * row_scale[pl.ds(scale_row, 64), :]
        scaled[pl.ds(row, 64), lanes(tile)] = weighted
        return (
            jnp.sum((value * value).reshape(8, 8, 128), axis=0),
            jnp.sum((weighted * weighted).reshape(8, 8, 128), axis=0),
        )

    def fold(value):
        return jnp.sum(value, axis=0, keepdims=True)

    def send(row, vector):
        for peer in range(8):
            sends[peer, row // 4, row % 4 : row % 4 + 1, :] = vector

    for tile in range(TILES_IN):
        plain, weighted = column(0, 0, tile)
        send(tile, fold(plain))
        send(16 + tile, fold(weighted))
    for tile in range(TILES_OUT):
        plain, weighted = column(64, 64, tile)
        for k in range(1, BLOCKS):
            more = column(64, 64 + 64 * k, k * TILES_OUT + tile)
            plain, weighted = plain + more[0], weighted + more[1]
        send(32 + tile, fold(plain))
        send(36 + tile, fold(weighted))


def column_sums_of(row_sums, rows_in, rows_out, summed):
    return pl.pallas_call(
        columns_kernel,
        out_shape=(
            jax.ShapeDtypeStruct(PACK, F32),
            jax.ShapeDtypeStruct((320, 128), F32),
            jax.ShapeDtypeStruct((1, ROWS_IN), F32),
            jax.ShapeDtypeStruct((1, ROWS_OUT), F32),
            jax.ShapeDtypeStruct((8, 10, 4, 128), F32),
        ),
        in_specs=[VMEM] * 4,
        out_specs=(VMEM,) * 5,
        compiler_params=PARAMS,
        name="column_sums",
    )(row_sums, rows_in, rows_out, summed)


def total_kernel(sums, sends):
    total = sums[0]
    for peer in range(1, 8):
        total = total + sums[peer]
    for peer in range(8):
        sends[peer] = total


def total_of(sums):
    return pl.pallas_call(
        total_kernel,
        out_shape=jax.ShapeDtypeStruct((8, 10, 4, 128), F32),
        in_specs=[VMEM],
        out_specs=VMEM,
        compiler_params=PARAMS,
        name="total",
    )(sums)


def factors_kernel(sums, cols_in, cols_out, sends):
    half = lax.axis_index("dp")
    total = sums[0]
    for peer in range(1, 8):
        total = total + sums[peer]
    energy_in = jnp.zeros((1, 128), F32)
    for part in range(4):
        new_in = DECAY * cols_in[half * 4 + part] + (1.0 - DECAY) * (total[part] * (1.0 / D) + EPSILON)
        energy_in += jnp.sum(total[4 + part] / new_in, axis=0, keepdims=True)
        for peer in range(8):
            sends[peer, part] = new_in
    new_out = DECAY * cols_out[half] + (1.0 - DECAY) * (total[8] * (1.0 / FF) + EPSILON)
    energy_out = jnp.sum(total[9] / new_out, axis=0, keepdims=True)
    last = jnp.concatenate([energy_in, energy_out, jnp.zeros((2, 128), F32)], axis=0)
    for peer in range(8):
        sends[peer, 4] = new_out
        sends[peer, 5] = last


def factors_of(sums, cols_in, cols_out):
    return pl.pallas_call(
        factors_kernel,
        out_shape=jax.ShapeDtypeStruct((8, 6, 4, 128), F32),
        in_specs=[VMEM] * 3,
        out_specs=VMEM,
        compiler_params=PARAMS,
        name="column_factors",
    )(sums, cols_in, cols_out)


def scales_kernel(factors, cols, scales):
    my_x = lax.axis_index("x")
    energies = factors[0, 5]
    for peer in range(1, 8):
        energies = energies + factors[peer, 5]

    def limit(row):
        energy = jnp.sum(energies[row : row + 1, :], axis=1, keepdims=True)
        return 1.0 / jnp.maximum(1.0, jnp.sqrt(energy * (1.0 / (D * FF))))

    limit_in, limit_out = limit(0), limit(1)
    for half in range(2):
        owner = my_x * 2 + half
        for part in range(4):
            here = factors[owner, part]
            cols[pl.ds(half * 16 + part * 4, 4), :] = here
            scales[pl.ds(half * 16 + part * 4, 4), :] = lax.rsqrt(here) * limit_in
        here = factors[owner, 4]
        cols[pl.ds(32 + half * 4, 4), :] = here
        scales[pl.ds(32 + half * 4, 4), :] = lax.rsqrt(here) * limit_out


def scales_of(factors):
    return pl.pallas_call(
        scales_kernel,
        out_shape=(jax.ShapeDtypeStruct((40, 128), F32), jax.ShapeDtypeStruct((40, 128), F32)),
        in_specs=[VMEM],
        out_specs=(VMEM, VMEM),
        compiler_params=PARAMS,
        name="scales",
    )(factors)


def update_kernel(
    cols, scales, scaled, row_scale, first, received, rows_in_new, rows_out_new,
    update_in, update_out, rows_in, rows_out, cols_in, cols_out,
    buf_in, buf_out, sems,
):
    own_half = lax.axis_index("dp")
    copies = []

    def write(source, target):
        copy = pltpu.make_async_copy(source, target, sems.at[len(copies)])
        copy.start()
        copies.append(copy)

    def block(buffer, target, offset, width, start):
        write(
            buffer.at[:, pl.ds(start, width)],
            target.at[:, pl.ds(pl.multiple_of(offset + start, 128), width)],
        )

    write(cols.at[0:32, :], cols_in)
    write(cols.at[32:40, :], cols_out)
    write(rows_in_new, rows_in)
    write(rows_out_new, rows_out)
    for which, half in ((0, own_half), (1, 1 - own_half)):

        def value(row, scale_row, tile):
            if which == 0:
                return scaled[pl.ds(row, 64), lanes(tile)]
            both = first[pl.ds(row, 64), lanes(tile)] + received[pl.ds(row, 64), lanes(tile)]
            return both * row_scale[pl.ds(scale_row, 64), :]

        for tile in range(TILES_IN):
            buf_in[which, :, lanes(tile)] = value(0, 0, tile) * scales[pl.ds(half * TILES_IN + tile, 1), :]
            if tile % 8 == 7:
                block(buf_in.at[which], update_in, half * HALF_IN, 1024, (tile - 7) * 128)
        for tile in range(TILES_OUT):
            scale = scales[pl.ds(32 + half * TILES_OUT + tile, 1), :]
            for k in range(BLOCKS):
                buf_out[which, pl.ds(64 * k, 64), lanes(tile)] = (
                    value(64, 64 + 64 * k, k * TILES_OUT + tile) * scale
                )
            if tile % 2 == 1:
                block(buf_out.at[which], update_out, half * HALF_OUT, 256, (tile - 1) * 128)
    for copy in copies:
        copy.wait()


def update_of(*operands):
    return pl.pallas_call(
        update_kernel,
        out_shape=(
            jax.ShapeDtypeStruct((ROWS_IN, COLS_IN), F32),
            jax.ShapeDtypeStruct((ROWS_OUT, COLS_OUT), F32),
            jax.ShapeDtypeStruct((1, ROWS_IN), F32),
            jax.ShapeDtypeStruct((1, ROWS_OUT), F32),
            jax.ShapeDtypeStruct((COLS_IN // 128, 128), F32),
            jax.ShapeDtypeStruct((COLS_OUT // 128, 128), F32),
        ),
        in_specs=[VMEM] * 8,
        out_specs=(HBM,) * 6,
        scratch_shapes=[
            pltpu.VMEM((2, ROWS_IN, HALF_IN), F32),
            pltpu.VMEM((2, ROWS_OUT, HALF_OUT), F32),
            pltpu.SemaphoreType.DMA((12,)),
        ],
        compiler_params=PARAMS,
        name="update",
    )(*operands)


def keep_in_hbm(x):
    return pltpu.with_memory_space_constraint(x, pltpu.HBM)


def per_device(grad_in, grad_out, rows_in, cols_in, rows_out, cols_out):
    swap = [(0, 1), (1, 0)]
    grad_in, grad_out = grad_in[0], grad_out[0]
    first, rows_in, rows_out, cols_in, cols_out = fetch(
        *map(
            keep_in_hbm,
            (
                grad_in,
                grad_out,
                rows_in.reshape(1, ROWS_IN),
                rows_out.reshape(1, ROWS_OUT),
                cols_in.reshape(8, 4, 128),
                cols_out.reshape(2, 4, 128),
            ),
        )
    )
    arrived_own = lax.ppermute(first, "dp", swap)
    own = widen_own(grad_in, grad_out)
    arrived_other = lax.ppermute(own, "dp", swap)

    summed, row_sums = row_sums_of(own, arrived_own)
    row_sums = lax.all_to_all(row_sums, ("x", "dp"), 0, 0)
    scaled, row_scale, new_rows_in, new_rows_out, sums = column_sums_of(row_sums, rows_in, rows_out, summed)
    sums = lax.all_to_all(sums, "y", 0, 0)
    sums = lax.all_to_all(total_of(sums), "z", 0, 0)
    factors = lax.all_to_all(factors_of(sums, cols_in, cols_out), ("x", "dp"), 0, 0)
    cols, scales = scales_of(factors)
    update_in, update_out, new_rows_in, new_rows_out, new_cols_in, new_cols_out = update_of(
        cols, scales, scaled, row_scale, first, arrived_other, new_rows_in, new_rows_out
    )
    return (
        update_in,
        update_out,
        new_rows_in.reshape(ROWS_IN),
        new_cols_in.reshape(COLS_IN),
        new_rows_out.reshape(ROWS_OUT),
        new_cols_out.reshape(COLS_OUT),
    )


def solution(mesh):
    fine = Mesh(mesh.devices.reshape(2, 8, 8, 4), ("dp", "z", "y", "x"))
    row = ("z", "y")
    return jax.shard_map(
        per_device,
        mesh=fine,
        in_specs=(
            P("dp", row, "x"),
            P("dp", row, "x"),
            P(row),
            P("x"),
            P(row),
            P("x"),
        ),
        out_specs=(P(row, "x"), P(row, "x"), P(row), P("x"), P(row), P("x")),
        check_vma=False,
    )
```

```python
import jax
import jax.numpy as jnp
from jax import lax
from jax.experimental import pallas as pl
from jax.experimental.pallas import tpu as pltpu
from jax.sharding import Mesh, PartitionSpec as P

D = 4096
FF = 16384

EPSILON = 1e-30
DECAY = 1.0 - 100.0 ** (-0.8)

ROWS_IN, COLS_IN = 64, 4096
ROWS_OUT, COLS_OUT = 256, 1024
HALF_IN, HALF_OUT = COLS_IN // 2, COLS_OUT // 2
PACK = (128, 2048)
BLOCKS = ROWS_OUT // 64
TILES_IN = HALF_IN // 128
TILES_OUT = HALF_OUT // 128

F32 = jnp.float32
VMEM = pl.BlockSpec(memory_space=pltpu.VMEM)
HBM = pl.BlockSpec(memory_space=pltpu.HBM)
PARAMS = pltpu.CompilerParams(vmem_limit_bytes=16 * 1024 * 1024)


def lanes(tile):
    return pl.ds(tile * 128, 128)


def half_copies(grad_in, grad_out, half, block_in, block_out, sems):
    columns_in = pl.ds(pl.multiple_of(half * HALF_IN, 128), HALF_IN)
    columns_out = pl.ds(pl.multiple_of(half * HALF_OUT, 128), HALF_OUT)
    return (
        pltpu.make_async_copy(grad_in.at[:, columns_in], block_in, sems.at[0]),
        pltpu.make_async_copy(grad_out.at[:, columns_out], block_out, sems.at[1]),
    )


HALF_SCRATCH = [
    pltpu.VMEM((ROWS_IN, HALF_IN), jnp.bfloat16),
    pltpu.VMEM((ROWS_OUT, HALF_OUT), jnp.bfloat16),
]


def fetch_kernel(grad_in, grad_out, *refs):
    first, other_in, other_out, sems = refs[2], refs[5], refs[6], refs[7]
    copies = half_copies(grad_in, grad_out, 1 - lax.axis_index("dp"), other_in, other_out, sems)
    small = [pltpu.make_async_copy(refs[at], refs[3 + at], sems.at[2 + at]) for at in range(2)]
    for copy in copies:
        copy.start(priority=1)
    for copy in small:
        copy.start()
    copies[0].wait()
    first[0:64, :] = other_in[...].astype(F32)
    copies[1].wait()
    for k in range(BLOCKS):
        first[64:128, pl.ds(k * HALF_OUT, HALF_OUT)] = other_out[pl.ds(64 * k, 64), :].astype(F32)
    for copy in small:
        copy.wait()


def fetch(grad_in, grad_out, *factors):
    return pl.pallas_call(
        fetch_kernel,
        out_shape=tuple(jax.ShapeDtypeStruct(shape, F32) for shape in (PACK, *(x.shape for x in factors))),
        in_specs=[HBM] * 4,
        out_specs=(VMEM,) * 3,
        scratch_shapes=HALF_SCRATCH + [pltpu.SemaphoreType.DMA((4,))],
        compiler_params=PARAMS,
        name="fetch",
    )(grad_in, grad_out, *factors)


def widen_kernel(grad_in, grad_out, packed):
    half = lax.axis_index("dp")
    packed[0:64, :] = grad_in[:, pl.ds(pl.multiple_of(half * HALF_IN, 128), HALF_IN)].astype(F32)
    columns = pl.ds(pl.multiple_of(half * HALF_OUT, 128), HALF_OUT)
    for k in range(BLOCKS):
        packed[64:128, pl.ds(k * HALF_OUT, HALF_OUT)] = grad_out[pl.ds(64 * k, 64), columns].astype(F32)


def widen_own(grad_in, grad_out):
    return pl.pallas_call(
        widen_kernel,
        out_shape=jax.ShapeDtypeStruct(PACK, F32),
        in_specs=[VMEM] * 2,
        out_specs=VMEM,
        compiler_params=PARAMS,
        name="widen_own",
    )(grad_in, grad_out)


def rows_kernel(own, received, summed, row_sums):
    def lane_partial(row, tiles):
        total = None
        for tile in tiles:
            value = own[pl.ds(row, 64), lanes(tile)] + received[pl.ds(row, 64), lanes(tile)]
            summed[pl.ds(row, 64), lanes(tile)] = value
            square = value * value
            total = square if total is None else total + square
        return total

    def to_lanes(upper, lower):
        return jnp.sum(jnp.concatenate([upper, lower], axis=0).T, axis=0, keepdims=True)

    part = lane_partial(0, range(TILES_IN))
    vectors = [to_lanes(part, jnp.zeros_like(part))]
    for pair in range(BLOCKS // 2):
        upper, lower = (
            lane_partial(64, range(k * TILES_OUT, (k + 1) * TILES_OUT)) for k in (2 * pair, 2 * pair + 1)
        )
        vectors.append(to_lanes(upper, lower))
    for at, vector in enumerate(vectors):
        for peer in range(8):
            row_sums[peer, :, lanes(at)] = vector


def row_sums_of(own, received):
    return pl.pallas_call(
        rows_kernel,
        out_shape=(jax.ShapeDtypeStruct(PACK, F32), jax.ShapeDtypeStruct((8, 1, 384), F32)),
        in_specs=[VMEM, VMEM],
        out_specs=(VMEM, VMEM),
        compiler_params=PARAMS,
        name="row_sums",
    )(own, received)


def columns_kernel(row_sums, rows_in, rows_out, summed, scaled, row_scale, new_in, new_out, sends):
    total = jnp.sum(row_sums[...], axis=0)
    fresh_in = DECAY * rows_in[...] + (1.0 - DECAY) * (total[:, 0:64] * (1.0 / FF) + EPSILON)
    fresh_out = DECAY * rows_out[...] + (1.0 - DECAY) * (total[:, 128:384] * (1.0 / D) + EPSILON)
    new_in[...] = fresh_in
    new_out[...] = fresh_out
    root_in = lax.rsqrt(fresh_in)
    root_out = lax.rsqrt(fresh_out)

    def to_rows(vector):
        return jnp.broadcast_to(vector, (128, 128)).T

    row_scale[0:64, :] = to_rows(jnp.concatenate([root_in, root_in], axis=1))[0:64, :]
    row_scale[64:192, :] = to_rows(root_out[:, 0:128])
    row_scale[192:320, :] = to_rows(root_out[:, 128:256])

    def column(row, scale_row, tile):
        value = summed[pl.ds(row, 64), lanes(tile)]
        weighted = value * row_scale[pl.ds(scale_row, 64), :]
        scaled[pl.ds(row, 64), lanes(tile)] = weighted
        return (
            jnp.sum((value * value).reshape(8, 8, 128), axis=0),
            jnp.sum((weighted * weighted).reshape(8, 8, 128), axis=0),
        )

    def fold(value):
        return jnp.sum(value, axis=0, keepdims=True)

    def send(chunk, row, vector):
        for peer in range(4 * chunk, 4 * chunk + 4):
            sends[peer, row // 4, row % 4 : row % 4 + 1, :] = vector

    for tile in range(TILES_IN):
        plain, weighted = column(0, 0, tile)
        send(tile // 8, tile % 8, fold(plain))
        send(tile // 8, 8 + tile % 8, fold(weighted))
    for tile in range(TILES_OUT):
        plain, weighted = column(64, 64, tile)
        for k in range(1, BLOCKS):
            more = column(64, 64 + 64 * k, k * TILES_OUT + tile)
            plain, weighted = plain + more[0], weighted + more[1]
        send(tile // 2, 16 + tile % 2, fold(plain))
        send(tile // 2, 18 + tile % 2, fold(weighted))


def column_sums_of(row_sums, rows_in, rows_out, summed):
    return pl.pallas_call(
        columns_kernel,
        out_shape=(
            jax.ShapeDtypeStruct(PACK, F32),
            jax.ShapeDtypeStruct((320, 128), F32),
            jax.ShapeDtypeStruct((1, ROWS_IN), F32),
            jax.ShapeDtypeStruct((1, ROWS_OUT), F32),
            jax.ShapeDtypeStruct((8, 5, 4, 128), F32),
        ),
        in_specs=[VMEM] * 4,
        out_specs=(VMEM,) * 5,
        compiler_params=PARAMS,
        name="column_sums",
    )(row_sums, rows_in, rows_out, summed)


def total_kernel(sums, sends):
    total = sums[0]
    for peer in range(1, 8):
        total = total + sums[peer]
    for peer in range(8):
        sends[peer] = total


def total_of(sums):
    return pl.pallas_call(
        total_kernel,
        out_shape=jax.ShapeDtypeStruct((8, 5, 4, 128), F32),
        in_specs=[VMEM],
        out_specs=VMEM,
        compiler_params=PARAMS,
        name="total",
    )(sums)


def factors_kernel(sums, cols_in, cols_out, sends):
    chunk = lax.axis_index("dp") * 2 + lax.axis_index("pair")
    total = sums[0]
    for peer in range(1, 8):
        total = total + sums[peer]
    energy_in = jnp.zeros((1, 128), F32)
    for part in range(2):
        new_in = DECAY * cols_in[chunk * 2 + part] + (1.0 - DECAY) * (total[part] * (1.0 / D) + EPSILON)
        energy_in += jnp.sum(total[2 + part] / new_in, axis=0, keepdims=True)
        for peer in range(16):
            sends[peer, part] = new_in
    new_out = DECAY * cols_out[chunk] + (1.0 - DECAY) * (total[4, 0:2] * (1.0 / FF) + EPSILON)
    energy_out = jnp.sum(total[4, 2:4] / new_out, axis=0, keepdims=True)
    last = jnp.concatenate([new_out, energy_in, energy_out], axis=0)
    for peer in range(16):
        sends[peer, 2] = last


def factors_of(sums, cols_in, cols_out):
    return pl.pallas_call(
        factors_kernel,
        out_shape=jax.ShapeDtypeStruct((16, 3, 4, 128), F32),
        in_specs=[VMEM] * 3,
        out_specs=VMEM,
        compiler_params=PARAMS,
        name="column_factors",
    )(sums, cols_in, cols_out)


def scales_kernel(factors, cols, scales):
    my_x = lax.axis_index("x")
    energies = factors[0, 2]
    for peer in range(1, 16):
        energies = energies + factors[peer, 2]

    def limit(row):
        energy = jnp.sum(energies[row : row + 1, :], axis=1, keepdims=True)
        return 1.0 / jnp.maximum(1.0, jnp.sqrt(energy * (1.0 / (D * FF))))

    limit_in, limit_out = limit(2), limit(3)
    for chunk in range(4):
        owner = my_x * 4 + chunk % 2 * 2 + chunk // 2
        for part in range(2):
            here = factors[owner, part]
            cols[pl.ds(chunk * 8 + part * 4, 4), :] = here
            scales[pl.ds(chunk * 8 + part * 4, 4), :] = lax.rsqrt(here) * limit_in
        here = factors[owner, 2, 0:2, :]
        cols[pl.ds(32 + chunk * 2, 2), :] = here
        scales[pl.ds(32 + chunk * 2, 2), :] = lax.rsqrt(here) * limit_out


def scales_of(factors):
    return pl.pallas_call(
        scales_kernel,
        out_shape=(jax.ShapeDtypeStruct((40, 128), F32), jax.ShapeDtypeStruct((40, 128), F32)),
        in_specs=[VMEM],
        out_specs=(VMEM, VMEM),
        compiler_params=PARAMS,
        name="scales",
    )(factors)


def update_kernel(
    cols, scales, scaled, row_scale, first, received, rows_in_new, rows_out_new,
    update_in, update_out, rows_in, rows_out, cols_in, cols_out,
    buf_in, buf_out, sems,
):
    own_half = lax.axis_index("dp")
    copies = []

    def write(source, target):
        copy = pltpu.make_async_copy(source, target, sems.at[len(copies)])
        copy.start()
        copies.append(copy)

    def block(buffer, target, offset, width, start):
        write(
            buffer.at[:, pl.ds(start, width)],
            target.at[:, pl.ds(pl.multiple_of(offset + start, 128), width)],
        )

    write(cols.at[0:32, :], cols_in)
    write(cols.at[32:40, :], cols_out)
    write(rows_in_new, rows_in)
    write(rows_out_new, rows_out)
    for which, half in ((0, own_half), (1, 1 - own_half)):

        def value(row, scale_row, tile):
            if which == 0:
                return scaled[pl.ds(row, 64), lanes(tile)]
            both = first[pl.ds(row, 64), lanes(tile)] + received[pl.ds(row, 64), lanes(tile)]
            return both * row_scale[pl.ds(scale_row, 64), :]

        for tile in range(TILES_IN):
            buf_in[which, :, lanes(tile)] = value(0, 0, tile) * scales[pl.ds(half * TILES_IN + tile, 1), :]
            if tile % 8 == 7:
                block(buf_in.at[which], update_in, half * HALF_IN, 1024, (tile - 7) * 128)
        for tile in range(TILES_OUT):
            scale = scales[pl.ds(32 + half * TILES_OUT + tile, 1), :]
            for k in range(BLOCKS):
                buf_out[which, pl.ds(64 * k, 64), lanes(tile)] = (
                    value(64, 64 + 64 * k, k * TILES_OUT + tile) * scale
                )
            if tile % 2 == 1:
                block(buf_out.at[which], update_out, half * HALF_OUT, 256, (tile - 1) * 128)
    for copy in copies:
        copy.wait()


def update_of(*operands):
    return pl.pallas_call(
        update_kernel,
        out_shape=(
            jax.ShapeDtypeStruct((ROWS_IN, COLS_IN), F32),
            jax.ShapeDtypeStruct((ROWS_OUT, COLS_OUT), F32),
            jax.ShapeDtypeStruct((1, ROWS_IN), F32),
            jax.ShapeDtypeStruct((1, ROWS_OUT), F32),
            jax.ShapeDtypeStruct((COLS_IN // 128, 128), F32),
            jax.ShapeDtypeStruct((COLS_OUT // 128, 128), F32),
        ),
        in_specs=[VMEM] * 8,
        out_specs=(HBM,) * 6,
        scratch_shapes=[
            pltpu.VMEM((2, ROWS_IN, HALF_IN), F32),
            pltpu.VMEM((2, ROWS_OUT, HALF_OUT), F32),
            pltpu.SemaphoreType.DMA((12,)),
        ],
        compiler_params=PARAMS,
        name="update",
    )(*operands)


def keep_in_hbm(x):
    return pltpu.with_memory_space_constraint(x, pltpu.HBM)


def per_device(grad_in, grad_out, rows_in, cols_in, rows_out, cols_out):
    swap = [(0, 1), (1, 0)]
    grad_in, grad_out = grad_in[0], grad_out[0]
    first, rows_in, rows_out = fetch(
        *map(
            keep_in_hbm,
            (
                grad_in,
                grad_out,
                rows_in.reshape(1, ROWS_IN),
                rows_out.reshape(1, ROWS_OUT),
            ),
        )
    )
    arrived_own = lax.ppermute(first, "dp", swap)
    own = widen_own(grad_in, grad_out)
    arrived_other = lax.ppermute(own, "dp", swap)

    summed, row_sums = row_sums_of(own, arrived_own)
    row_sums = lax.all_to_all(row_sums, ("x", "dp"), 0, 0)
    scaled, row_scale, new_rows_in, new_rows_out, sums = column_sums_of(row_sums, rows_in, rows_out, summed)
    sums = lax.all_to_all(sums, ("pair", "y"), 0, 0)
    sums = lax.all_to_all(total_of(sums), "z", 0, 0)
    factors = factors_of(sums, cols_in.reshape(8, 4, 128), cols_out.reshape(4, 2, 128))
    factors = lax.all_to_all(factors, ("x", "pair", "dp"), 0, 0)
    cols, scales = scales_of(factors)
    update_in, update_out, new_rows_in, new_rows_out, new_cols_in, new_cols_out = update_of(
        cols, scales, scaled, row_scale, first, arrived_other, new_rows_in, new_rows_out
    )
    return (
        update_in,
        update_out,
        new_rows_in.reshape(ROWS_IN),
        new_cols_in.reshape(COLS_IN),
        new_rows_out.reshape(ROWS_OUT),
        new_cols_out.reshape(COLS_OUT),
    )


def solution(mesh):
    fine = Mesh(mesh.devices.reshape(2, 8, 4, 2, 4), ("dp", "z", "y", "pair", "x"))
    row = ("z", "y", "pair")
    return jax.shard_map(
        per_device,
        mesh=fine,
        in_specs=(
            P("dp", row, "x"),
            P("dp", row, "x"),
            P(row),
            P("x"),
            P(row),
            P("x"),
        ),
        out_specs=(P(row, "x"), P(row, "x"), P(row), P("x"), P(row), P("x")),
        check_vma=False,
    )
```

```python
import jax
import jax.numpy as jnp
from jax import lax
from jax.experimental import pallas as pl
from jax.experimental.pallas import tpu as pltpu
from jax.sharding import Mesh, PartitionSpec as P

D = 4096
FF = 16384

EPSILON = 1e-30
DECAY = 1.0 - 100.0 ** (-0.8)

ROWS_IN, COLS_IN = 64, 4096
ROWS_OUT, COLS_OUT = 256, 1024
HALF_IN, HALF_OUT = COLS_IN // 2, COLS_OUT // 2
PACK = (128, 2048)
BLOCKS = ROWS_OUT // 64
TILES_IN = HALF_IN // 128
TILES_OUT = HALF_OUT // 128

F32 = jnp.float32
VMEM = pl.BlockSpec(memory_space=pltpu.VMEM)
HBM = pl.BlockSpec(memory_space=pltpu.HBM)
PARAMS = pltpu.CompilerParams(vmem_limit_bytes=16 * 1024 * 1024)


def lanes(tile):
    return pl.ds(tile * 128, 128)


def half_copies(grad_in, grad_out, half, block_in, block_out, sems):
    columns_in = pl.ds(pl.multiple_of(half * HALF_IN, 128), HALF_IN)
    columns_out = pl.ds(pl.multiple_of(half * HALF_OUT, 128), HALF_OUT)
    return (
        pltpu.make_async_copy(grad_in.at[:, columns_in], block_in, sems.at[0]),
        pltpu.make_async_copy(grad_out.at[:, columns_out], block_out, sems.at[1]),
    )


HALF_SCRATCH = [
    pltpu.VMEM((ROWS_IN, HALF_IN), jnp.bfloat16),
    pltpu.VMEM((ROWS_OUT, HALF_OUT), jnp.bfloat16),
]


def fetch_kernel(grad_in, grad_out, *refs):
    first, other_in, other_out, sems = refs[4], refs[9], refs[10], refs[11]
    copies = half_copies(grad_in, grad_out, 1 - lax.axis_index("dp"), other_in, other_out, sems)
    small = [pltpu.make_async_copy(refs[at], refs[5 + at], sems.at[2 + at]) for at in range(4)]
    for copy in (*copies, *small):
        copy.start()
    copies[0].wait()
    first[0:64, :] = other_in[...].astype(F32)
    copies[1].wait()
    for k in range(BLOCKS):
        first[64:128, pl.ds(k * HALF_OUT, HALF_OUT)] = other_out[pl.ds(64 * k, 64), :].astype(F32)
    for copy in small:
        copy.wait()


def fetch(grad_in, grad_out, *factors):
    return pl.pallas_call(
        fetch_kernel,
        out_shape=tuple(jax.ShapeDtypeStruct(shape, F32) for shape in (PACK, *(x.shape for x in factors))),
        in_specs=[HBM] * 6,
        out_specs=(VMEM,) * 5,
        scratch_shapes=HALF_SCRATCH + [pltpu.SemaphoreType.DMA((6,))],
        compiler_params=PARAMS,
        name="fetch",
    )(grad_in, grad_out, *factors)


def widen_kernel(grad_in, grad_out, packed):
    half = lax.axis_index("dp")
    packed[0:64, :] = grad_in[:, pl.ds(pl.multiple_of(half * HALF_IN, 128), HALF_IN)].astype(F32)
    columns = pl.ds(pl.multiple_of(half * HALF_OUT, 128), HALF_OUT)
    for k in range(BLOCKS):
        packed[64:128, pl.ds(k * HALF_OUT, HALF_OUT)] = grad_out[pl.ds(64 * k, 64), columns].astype(F32)


def widen_own(grad_in, grad_out):
    return pl.pallas_call(
        widen_kernel,
        out_shape=jax.ShapeDtypeStruct(PACK, F32),
        in_specs=[VMEM] * 2,
        out_specs=VMEM,
        compiler_params=PARAMS,
        name="widen_own",
    )(grad_in, grad_out)


def rows_kernel(own, received, summed, row_sums):
    def lane_partial(row, tiles):
        total = None
        for tile in tiles:
            value = own[pl.ds(row, 64), lanes(tile)] + received[pl.ds(row, 64), lanes(tile)]
            summed[pl.ds(row, 64), lanes(tile)] = value
            square = value * value
            total = square if total is None else total + square
        return total

    def to_lanes(upper, lower):
        return jnp.sum(jnp.concatenate([upper, lower], axis=0).T, axis=0, keepdims=True)

    part = lane_partial(0, range(TILES_IN))
    vectors = [to_lanes(part, jnp.zeros_like(part))]
    for pair in range(BLOCKS // 2):
        upper, lower = (
            lane_partial(64, range(k * TILES_OUT, (k + 1) * TILES_OUT)) for k in (2 * pair, 2 * pair + 1)
        )
        vectors.append(to_lanes(upper, lower))
    for at, vector in enumerate(vectors):
        for peer in range(8):
            row_sums[peer, :, lanes(at)] = vector


def row_sums_of(own, received):
    return pl.pallas_call(
        rows_kernel,
        out_shape=(jax.ShapeDtypeStruct(PACK, F32), jax.ShapeDtypeStruct((8, 1, 384), F32)),
        in_specs=[VMEM, VMEM],
        out_specs=(VMEM, VMEM),
        compiler_params=PARAMS,
        name="row_sums",
    )(own, received)


def columns_kernel(row_sums, rows_in, rows_out, summed, scaled, row_scale, new_in, new_out, sends):
    total = jnp.sum(row_sums[...], axis=0)
    fresh_in = DECAY * rows_in[...] + (1.0 - DECAY) * (total[:, 0:64] * (1.0 / FF) + EPSILON)
    fresh_out = DECAY * rows_out[...] + (1.0 - DECAY) * (total[:, 128:384] * (1.0 / D) + EPSILON)
    new_in[...] = fresh_in
    new_out[...] = fresh_out
    root_in = lax.rsqrt(fresh_in)
    root_out = lax.rsqrt(fresh_out)

    def to_rows(vector):
        return jnp.broadcast_to(vector, (128, 128)).T

    row_scale[0:64, :] = to_rows(jnp.concatenate([root_in, root_in], axis=1))[0:64, :]
    row_scale[64:192, :] = to_rows(root_out[:, 0:128])
    row_scale[192:320, :] = to_rows(root_out[:, 128:256])

    def column(row, scale_row, tile):
        value = summed[pl.ds(row, 64), lanes(tile)]
        weighted = value * row_scale[pl.ds(scale_row, 64), :]
        scaled[pl.ds(row, 64), lanes(tile)] = weighted
        return (
            jnp.sum((value * value).reshape(8, 8, 128), axis=0),
            jnp.sum((weighted * weighted).reshape(8, 8, 128), axis=0),
        )

    def fold(value):
        return jnp.sum(value, axis=0, keepdims=True)

    def send(chunk, row, vector):
        for peer in range(4 * chunk, 4 * chunk + 4):
            sends[peer, row // 4, row % 4 : row % 4 + 1, :] = vector

    for tile in range(TILES_IN):
        plain, weighted = column(0, 0, tile)
        send(tile // 8, tile % 8, fold(plain))
        send(tile // 8, 8 + tile % 8, fold(weighted))
    for tile in range(TILES_OUT):
        plain, weighted = column(64, 64, tile)
        for k in range(1, BLOCKS):
            more = column(64, 64 + 64 * k, k * TILES_OUT + tile)
            plain, weighted = plain + more[0], weighted + more[1]
        send(tile // 2, 16 + tile % 2, fold(plain))
        send(tile // 2, 18 + tile % 2, fold(weighted))


def column_sums_of(row_sums, rows_in, rows_out, summed):
    return pl.pallas_call(
        columns_kernel,
        out_shape=(
            jax.ShapeDtypeStruct(PACK, F32),
            jax.ShapeDtypeStruct((320, 128), F32),
            jax.ShapeDtypeStruct((1, ROWS_IN), F32),
            jax.ShapeDtypeStruct((1, ROWS_OUT), F32),
            jax.ShapeDtypeStruct((8, 5, 4, 128), F32),
        ),
        in_specs=[VMEM] * 4,
        out_specs=(VMEM,) * 5,
        compiler_params=PARAMS,
        name="column_sums",
    )(row_sums, rows_in, rows_out, summed)


def total_kernel(sums, sends):
    total = sums[0]
    for peer in range(1, 8):
        total = total + sums[peer]
    for quarter in range(2):
        rest = jnp.concatenate([total[4, quarter : quarter + 1], total[4, 2 + quarter : 3 + quarter]], axis=0)
        for peer in range(4 * quarter, 4 * quarter + 4):
            sends[peer, 0] = total[quarter]
            sends[peer, 1] = total[2 + quarter]
            sends[peer, 2] = jnp.concatenate([rest, rest], axis=0)


def total_of(sums):
    return pl.pallas_call(
        total_kernel,
        out_shape=jax.ShapeDtypeStruct((8, 3, 4, 128), F32),
        in_specs=[VMEM],
        out_specs=VMEM,
        compiler_params=PARAMS,
        name="total",
    )(sums)


def factors_kernel(sums, cols_in, cols_out, sends):
    chunk = (lax.axis_index("dp") * 2 + lax.axis_index("zpair")) * 2 + lax.axis_index("ypair")
    total = sums[0]
    for peer in range(1, 8):
        total = total + sums[peer]
    new_in = DECAY * cols_in[chunk] + (1.0 - DECAY) * (total[0] * (1.0 / D) + EPSILON)
    energy_in = jnp.sum(total[1] / new_in, axis=0, keepdims=True)
    new_out = DECAY * cols_out[chunk] + (1.0 - DECAY) * (total[2, 0:1] * (1.0 / FF) + EPSILON)
    energy_out = total[2, 1:2] / new_out
    last = jnp.concatenate([new_out, energy_in, energy_out, jnp.zeros((1, 128), F32)], axis=0)
    for peer in range(32):
        sends[peer, 0] = new_in
        sends[peer, 1] = last


def factors_of(sums, cols_in, cols_out):
    return pl.pallas_call(
        factors_kernel,
        out_shape=jax.ShapeDtypeStruct((32, 2, 4, 128), F32),
        in_specs=[VMEM] * 3,
        out_specs=VMEM,
        compiler_params=PARAMS,
        name="column_factors",
    )(sums, cols_in, cols_out)


def scales_kernel(factors, cols, scales):
    my_x = lax.axis_index("x")
    energies = factors[0, 1]
    for peer in range(1, 32):
        energies = energies + factors[peer, 1]

    def limit(row):
        energy = jnp.sum(energies[row : row + 1, :], axis=1, keepdims=True)
        return 1.0 / jnp.maximum(1.0, jnp.sqrt(energy * (1.0 / (D * FF))))

    limit_in, limit_out = limit(1), limit(2)
    for chunk in range(8):
        owner = my_x * 8 + chunk % 4 * 2 + chunk // 4
        here = factors[owner, 0]
        cols[pl.ds(chunk * 4, 4), :] = here
        scales[pl.ds(chunk * 4, 4), :] = lax.rsqrt(here) * limit_in
        here = factors[owner, 1, 0:1, :]
        cols[pl.ds(32 + chunk, 1), :] = here
        scales[pl.ds(32 + chunk, 1), :] = lax.rsqrt(here) * limit_out


def scales_of(factors):
    return pl.pallas_call(
        scales_kernel,
        out_shape=(jax.ShapeDtypeStruct((40, 128), F32), jax.ShapeDtypeStruct((40, 128), F32)),
        in_specs=[VMEM],
        out_specs=(VMEM, VMEM),
        compiler_params=PARAMS,
        name="scales",
    )(factors)


def update_kernel(
    cols, scales, scaled, row_scale, first, received, rows_in_new, rows_out_new,
    update_in, update_out, rows_in, rows_out, cols_in, cols_out,
    buf_in, buf_out, sems,
):
    own_half = lax.axis_index("dp")
    copies = []

    def write(source, target):
        copy = pltpu.make_async_copy(source, target, sems.at[len(copies)])
        copy.start()
        copies.append(copy)

    def block(buffer, target, offset, width, start):
        write(
            buffer.at[:, pl.ds(start, width)],
            target.at[:, pl.ds(pl.multiple_of(offset + start, 128), width)],
        )

    write(cols.at[0:32, :], cols_in)
    write(cols.at[32:40, :], cols_out)
    write(rows_in_new, rows_in)
    write(rows_out_new, rows_out)
    for which, half in ((0, own_half), (1, 1 - own_half)):

        def value(row, scale_row, tile):
            if which == 0:
                return scaled[pl.ds(row, 64), lanes(tile)]
            both = first[pl.ds(row, 64), lanes(tile)] + received[pl.ds(row, 64), lanes(tile)]
            return both * row_scale[pl.ds(scale_row, 64), :]

        for tile in range(TILES_IN):
            buf_in[which, :, lanes(tile)] = value(0, 0, tile) * scales[pl.ds(half * TILES_IN + tile, 1), :]
            if tile % 8 == 7:
                block(buf_in.at[which], update_in, half * HALF_IN, 1024, (tile - 7) * 128)
        for tile in range(TILES_OUT):
            scale = scales[pl.ds(32 + half * TILES_OUT + tile, 1), :]
            for k in range(BLOCKS):
                buf_out[which, pl.ds(64 * k, 64), lanes(tile)] = (
                    value(64, 64 + 64 * k, k * TILES_OUT + tile) * scale
                )
            if tile % 2 == 1:
                block(buf_out.at[which], update_out, half * HALF_OUT, 256, (tile - 1) * 128)
    for copy in copies:
        copy.wait()


def update_of(*operands):
    return pl.pallas_call(
        update_kernel,
        out_shape=(
            jax.ShapeDtypeStruct((ROWS_IN, COLS_IN), F32),
            jax.ShapeDtypeStruct((ROWS_OUT, COLS_OUT), F32),
            jax.ShapeDtypeStruct((1, ROWS_IN), F32),
            jax.ShapeDtypeStruct((1, ROWS_OUT), F32),
            jax.ShapeDtypeStruct((COLS_IN // 128, 128), F32),
            jax.ShapeDtypeStruct((COLS_OUT // 128, 128), F32),
        ),
        in_specs=[VMEM] * 8,
        out_specs=(HBM,) * 6,
        scratch_shapes=[
            pltpu.VMEM((2, ROWS_IN, HALF_IN), F32),
            pltpu.VMEM((2, ROWS_OUT, HALF_OUT), F32),
            pltpu.SemaphoreType.DMA((12,)),
        ],
        compiler_params=PARAMS,
        name="update",
    )(*operands)


def keep_in_hbm(x):
    return pltpu.with_memory_space_constraint(x, pltpu.HBM)


def per_device(grad_in, grad_out, rows_in, cols_in, rows_out, cols_out):
    swap = [(0, 1), (1, 0)]
    grad_in, grad_out = grad_in[0], grad_out[0]
    first, rows_in, rows_out, cols_in, cols_out = fetch(
        *map(
            keep_in_hbm,
            (
                grad_in,
                grad_out,
                rows_in.reshape(1, ROWS_IN),
                rows_out.reshape(1, ROWS_OUT),
                cols_in.reshape(8, 4, 128),
                cols_out.reshape(8, 1, 128),
            ),
        )
    )
    arrived_own = lax.ppermute(first, "dp", swap)
    own = widen_own(grad_in, grad_out)
    arrived_other = lax.ppermute(own, "dp", swap)

    summed, row_sums = row_sums_of(own, arrived_own)
    row_sums = lax.all_to_all(row_sums, ("x", "dp"), 0, 0)
    scaled, row_scale, new_rows_in, new_rows_out, sums = column_sums_of(row_sums, rows_in, rows_out, summed)
    sums = lax.all_to_all(sums, ("zpair", "z"), 0, 0)
    sums = lax.all_to_all(total_of(sums), ("ypair", "y"), 0, 0)
    factors = lax.all_to_all(factors_of(sums, cols_in, cols_out), ("x", "zpair", "ypair", "dp"), 0, 0)
    cols, scales = scales_of(factors)
    update_in, update_out, new_rows_in, new_rows_out, new_cols_in, new_cols_out = update_of(
        cols, scales, scaled, row_scale, first, arrived_other, new_rows_in, new_rows_out
    )
    return (
        update_in,
        update_out,
        new_rows_in.reshape(ROWS_IN),
        new_cols_in.reshape(COLS_IN),
        new_rows_out.reshape(ROWS_OUT),
        new_cols_out.reshape(COLS_OUT),
    )


def solution(mesh):
    fine = Mesh(mesh.devices.reshape(2, 4, 2, 4, 2, 4), ("dp", "z", "zpair", "y", "ypair", "x"))
    row = ("z", "zpair", "y", "ypair")
    return jax.shard_map(
        per_device,
        mesh=fine,
        in_specs=(
            P("dp", row, "x"),
            P("dp", row, "x"),
            P(row),
            P("x"),
            P(row),
            P("x"),
        ),
        out_specs=(P(row, "x"), P(row, "x"), P(row), P("x"), P(row), P("x")),
        check_vma=False,
    )
```
